32 devices in a mesh: dp: 8 (over z, x), tensor: 4 (over y, core).
Axes of the slice: x: 2, y: 2, z: 4, core: 2. Of those that a mesh axis runs over, the one named last changes fastest.
Arguments:
- residual: bfloat16 [64, 64, 4096], P('dp', None, 'tensor'), may hold values from -128 to 128
- queries: bfloat16 [64, 64, 4096], P('dp', None, 'tensor'), may hold values from -30 to 30
- attn_keys: bfloat16 [64, 64, 512], P('dp', None, 'tensor'), may hold values from -6 to 6
- values: bfloat16 [64, 64, 512], P('dp', None, 'tensor'), may hold values from -6 to 6
- out_weight: bfloat16 [4096, 4096], P('tensor'), may hold values from -0.09375 to 0.09375
- norm_gain: float32 [4096], P('tensor'), may hold values from 0.1 to 1.9
- probe_weight: float32 [4096, 64], P('tensor'), may hold values from -0.09375 to 0.09375
- partner_slot: int32 [64], P('dp'), may hold values from 0 to 7, as said below
- patch_list: int32 [64, 64, 2], P('dp', 'tensor'), may hold values from 0 to 63, as said below
- concept_labels: int32 [64, 64], P('dp'), may hold values from 0 to 63
Outputs:
- attn_out: bfloat16 [64, 64, 4096], P('dp', None, 'tensor')
- logits: float32 [64, 64, 64], P('dp')
- probe_grad: float32 [4096, 64], P('tensor')
The draws below stay inside these ranges and needn't reach their ends.
Inputs may be any that keep to these rules, and one draw needn't show every extreme that they name: Prompt j of device i of dp, for i below 4, is paired with prompt partner_slot of it on device i + 4, and that prompt's partner_slot is j; on each device the values are a permutation. `patch_list`: each entry is (head, position). A prompt's list equals its partner's, entry for entry. Its entries are distinct, and entries k * 16 to (k + 1) * 16 - 1 name heads of the k-th block of 8 consecutive heads.
All inputs are finite; a program needn't handle non-finite values.
Results may differ from the reference program's by a relative error of at most 0.01.
Values may be sent and summed in bfloat16 or wider, within the bound.
A program may use at most 128 MiB of HBM per device.

```python
import math
import jax
import jax.numpy as jnp
from jax import lax

DW = 4096
HEADS = 32
KV = 4
HDIM = 128
LEN = 64
CONCEPTS = 64
KQ = 16
PROMPTS_DEV = 8
PROMPTS = 64
N_DP = 8
N_TENSOR = 4


def pairing(key):
    half_way = N_DP // 2
    base_key = jax.random.fold_in(key, 101)
    perms = jax.vmap(lambda index: jax.random.permutation(jax.random.fold_in(base_key, index), PROMPTS_DEV))(jnp.arange(half_way))
    perms = perms.astype(jnp.int32)
    counting = jnp.arange(PROMPTS_DEV, dtype=jnp.int32)
    inverse = jax.vmap(lambda order: jnp.zeros((PROMPTS_DEV,), jnp.int32).at[order].set(counting))(perms)
    return jnp.concatenate([perms, inverse], axis=0)


def draw_partner_slot(key, part):
    return pairing(key).reshape(PROMPTS).astype(jnp.int32)


def draw_patch_list(key, part):
    slots = pairing(key)
    half_way = N_DP // 2
    counting = jnp.arange(PROMPTS_DEV, dtype=jnp.int32)
    lower_ids = jnp.arange(half_way, dtype=jnp.int32)[:, None] * PROMPTS_DEV + counting[None, :]
    upper_ids = jnp.arange(half_way, dtype=jnp.int32)[:, None] * PROMPTS_DEV + slots[half_way:]
    pair_ids = jnp.concatenate([lower_ids, upper_ids], axis=0).reshape(PROMPTS)
    block_heads = HEADS // N_TENSOR
    base_key = jax.random.fold_in(key, 202)

    def entries(pair_index, block_index):
        order = jax.random.permutation(jax.random.fold_in(base_key, pair_index * N_TENSOR + block_index), block_heads * LEN)[:KQ]
        order = order.astype(jnp.int32)
        return jnp.stack([block_index * block_heads + order // LEN, order % LEN], axis=-1)
    blocks = jnp.arange(N_TENSOR, dtype=jnp.int32)
    table = jax.vmap(lambda pair_index: jax.vmap(lambda block_index: entries(pair_index, block_index))(blocks))(jnp.arange(half_way * PROMPTS_DEV, dtype=jnp.int32))
    return table[pair_ids].reshape(PROMPTS, N_TENSOR * KQ, 2).astype(jnp.int32)


def attention_pair(key):
    query_key = jax.random.fold_in(key, 301)
    key_key = jax.random.fold_in(key, 302)
    key_rows = jnp.clip(jax.random.normal(key_key, (PROMPTS, LEN, KV * HDIM), jnp.float32), -6.0, 6.0)
    query_rows = 2.0 * jnp.clip(jax.random.normal(query_key, (PROMPTS, LEN, HEADS * HDIM), jnp.float32), -6.0, 6.0)
    return (query_rows, key_rows)


def draw_queries(key, part):
    return attention_pair(key)[0].astype(jnp.bfloat16)


def draw_attn_keys(key, part):
    return attention_pair(key)[1].astype(jnp.bfloat16)


def draw_residual(key, part):
    noise_key = jax.random.fold_in(key, 401)
    row_key = jax.random.fold_in(key, 402)
    column_key = jax.random.fold_in(key, 403)
    shape = (PROMPTS, LEN, DW)
    column_log = jnp.arange(DW).astype(jnp.float32) / DW + jax.random.uniform(column_key, (DW,), jnp.float32, -0.15, 0.15)
    row_log = jax.random.uniform(row_key, (PROMPTS, LEN, 1), jnp.float32, 0.0, 1.0)
    noise = jnp.clip(jax.random.normal(noise_key, shape, jnp.float32), -6.0, 6.0)
    return (0.15 * noise * jnp.power(10.0, row_log) * jnp.power(10.0, column_log)).astype(jnp.bfloat16)


def with_ends(values, stream_key, smallest, largest):
    place = [jax.random.randint(jax.random.fold_in(stream_key, axis), (), 0, length) for axis, length in enumerate(values.shape)]
    longest = values.shape.index(max(values.shape))
    neighbour = place[:longest] + [(place[longest] + 1) % values.shape[longest]] + place[longest + 1:]
    return values.at[tuple(place)].set(smallest).at[tuple(neighbour)].set(largest)


def levels(own_key, extent, split, low, high):
    def one(dim, blocks):
        draws = jax.random.uniform(jax.random.fold_in(jax.random.fold_in(own_key, 6), dim), (blocks,), jnp.float32, low / len(split), high / len(split))
        return jnp.repeat(jnp.exp(draws), extent[dim] // blocks).reshape((-1,) + (1,) * (len(extent) - dim - 1))

    gain = one(*split[0])
    for cut in split[1:]:
        gain = gain * one(*cut)
    return gain


def centred(stream_key, dims, scale, limit, split=(), kind=jnp.bfloat16):
    drawn = scale * jax.random.normal(stream_key, dims, jnp.float32)
    if split:
        drawn = drawn * levels(stream_key, dims, split, -0.22, 0.18)
    return jnp.clip(drawn, -limit, limit).astype(kind)


def setup_inputs(seed: int = 0) -> dict:
    arg_keys = jax.random.split(jax.random.key(seed), 11)
    return {
        "residual": draw_residual(jax.random.fold_in(arg_keys[10], 71), 0),
        "queries": draw_queries(jax.random.fold_in(arg_keys[10], 71), 0),
        "attn_keys": draw_attn_keys(jax.random.fold_in(arg_keys[10], 71), 0),
        "values": centred(arg_keys[3], (PROMPTS, LEN, KV * HDIM), 1.0, 6.0, ((0, 8), (2, 4))),
        "out_weight": centred(arg_keys[4], (HEADS * HDIM, DW), (HEADS * HDIM) ** -0.5, 0.09375, ((0, 4),)),
        "norm_gain": jnp.clip(1.0 + 0.18 * jax.random.normal(arg_keys[5], (DW,), jnp.float32), 0.1, 1.9),
        "probe_weight": centred(arg_keys[6], (DW, CONCEPTS), DW ** -0.5, 0.09375, ((0, 4),), jnp.float32),
        "partner_slot": draw_partner_slot(jax.random.fold_in(arg_keys[10], 71), 0),
        "patch_list": draw_patch_list(jax.random.fold_in(arg_keys[10], 71), 0),
        "concept_labels": with_ends(jax.random.randint(arg_keys[9], (PROMPTS, LEN), 0, CONCEPTS), jax.random.fold_in(arg_keys[9], 1), 0, CONCEPTS - 1).astype(jnp.int32),
    }


norm_epsilon = 1e-05

def attend(queries, attn_keys, values):
    prompt_count = queries.shape[0]
    group_size = HEADS // KV
    query_blocks = queries.astype(jnp.float32).reshape(prompt_count, LEN, KV, group_size, HDIM)
    key_blocks = attn_keys.astype(jnp.float32).reshape(prompt_count, LEN, KV, HDIM)
    value_blocks = values.astype(jnp.float32).reshape(prompt_count, LEN, KV, HDIM)
    scores = jnp.einsum('pqkgd,pskd->pkgqs', query_blocks, key_blocks) / math.sqrt(HDIM)
    causal = jnp.arange(LEN)[:, None] >= jnp.arange(LEN)[None, :]
    scores = jnp.where(causal, scores, -jnp.inf)
    highest = lax.optimization_barrier(jnp.max(scores, axis=-1, keepdims=True))
    exponent = jnp.exp(scores - highest)
    weights = (exponent / lax.optimization_barrier(jnp.sum(exponent, axis=-1, keepdims=True))).astype(jnp.bfloat16)
    weights = lax.optimization_barrier(weights).astype(jnp.float32)
    mixed_rows = jnp.einsum('pkgqs,pskd->pqkgd', weights, value_blocks)
    return mixed_rows.reshape(prompt_count, LEN, HEADS, HDIM).astype(jnp.bfloat16)

def reference(residual, queries, attn_keys, values, out_weight, norm_gain, probe_weight, partner_slot, patch_list, concept_labels):
    heads_out = attend(queries, attn_keys, values)
    half_way = N_DP // 2
    prompt_ids = jnp.arange(PROMPTS, dtype=jnp.int32)
    partner_ids = ((prompt_ids // PROMPTS_DEV + half_way) % N_DP * PROMPTS_DEV + partner_slot).astype(jnp.int32)
    from_partner = heads_out[partner_ids]
    row_ids = jnp.broadcast_to(prompt_ids[:, None], patch_list.shape[:2])
    patch_mask = jnp.zeros((PROMPTS, LEN, HEADS), dtype=bool).at[row_ids, patch_list[..., 1], patch_list[..., 0]].set(True)
    patched = jnp.where(patch_mask[..., None], from_partner, heads_out)
    token_count = PROMPTS * LEN
    flat_heads = patched.reshape(token_count, HEADS * HDIM)
    block_rows = HEADS * HDIM // N_TENSOR
    total = jnp.zeros((token_count, DW), jnp.float32)
    for block_index in range(N_TENSOR):
        lower = block_index * block_rows
        partial_value = jnp.dot(flat_heads[:, lower:lower + block_rows], out_weight[lower:lower + block_rows], preferred_element_type=jnp.float32)
        partial_value = lax.optimization_barrier(partial_value.astype(jnp.bfloat16)).astype(jnp.float32)
        total = total + partial_value
    attn_out = total.astype(jnp.bfloat16)
    hidden = residual.reshape(token_count, DW).astype(jnp.float32) + attn_out.astype(jnp.float32)
    mean_square = lax.optimization_barrier(jnp.sum(hidden * hidden, axis=1, keepdims=True)) / DW
    normed = hidden * lax.rsqrt(mean_square + norm_epsilon) * norm_gain.astype(jnp.float32)
    logits = jnp.dot(normed, probe_weight, precision=lax.Precision.HIGHEST, preferred_element_type=jnp.float32)
    classes = jnp.arange(CONCEPTS, dtype=jnp.int32)
    target = (concept_labels.reshape(token_count)[:, None] == classes[None, :]).astype(jnp.float32)
    error = jax.nn.sigmoid(logits) - target
    probe_grad = jnp.dot(normed.T, error, precision=lax.Precision.HIGHEST, preferred_element_type=jnp.float32) / math.sqrt(token_count)
    return (attn_out.reshape(PROMPTS, LEN, DW), logits.reshape(PROMPTS, LEN, CONCEPTS), probe_grad)
```

```python
import functools
import math

import jax
import jax.numpy as jnp
from jax import lax
from jax.experimental import pallas as pl
from jax.experimental.pallas import tpu as pltpu
from jax.sharding import PartitionSpec as P

HDIM = 128
LANES = 128
norm_epsilon = 1e-05
MESH = pl.DeviceIdType.MESH
F32 = jnp.float32
BF16 = jnp.bfloat16


def contract(a, b, dim_a, dim_b):
    return lax.dot_general(
        a, b, (((dim_a,), (dim_b,)), ((), ())), preferred_element_type=F32
    )


def kernel(
    n_dp,
    width,
    slot_ref,
    q_ref,
    k_ref,
    v_ref,
    patch_ref,
    label_ref,
    gain_ref,
    probe_ref,
    weight_hbm,
    residual_hbm,
    out_hbm,
    logits_ref,
    grad_ref,
    w_buf,
    res_buf,
    out_buf,
    heads_buf,
    x_buf,
    entry_send,
    entry_recv,
    a_send,
    a_recv,
    c_send,
    c_recv,
    d_send,
    d_recv,
    own_buf,
    hg_buf,
    probe_buf,
    target_buf,
    err_buf,
    l1_send,
    l1_recv,
    l2_send,
    l2_recv,
    g_send,
    g_recv,
    ag_buf,
    w_sem,
    res_sem,
    out_sem,
    entry_sem,
    a_sems,
    c_sems,
    d_sems,
    l1_sems,
    l2_sems,
    rs_ssem,
    rs_rsem,
    ag_ssem,
    ag_rsem,
):
    prompts, length, features = q_ref.shape
    local_heads = features // HDIM
    classes = probe_ref.shape[1]
    block = res_buf.shape[2]
    d = lax.axis_index("dp")
    t = lax.axis_index("tensor")
    core = lax.rem(t, 2)
    sib = t + 1 - 2 * core
    opp = lax.rem(t + 2, 4)
    opp_sib = lax.rem(sib + 2, 4)
    partner = lax.rem(d + n_dp // 2, n_dp)

    barrier = pltpu.get_barrier_semaphore()
    pl.semaphore_signal(barrier, inc=1, device_id=(d, sib), device_id_type=MESH)
    pl.semaphore_signal(barrier, inc=1, device_id=(d, opp), device_id_type=MESH)
    for off in range(1, n_dp):
        pl.semaphore_signal(
            barrier, inc=1, device_id=(lax.rem(d + off, n_dp), t), device_id_type=MESH
        )

    w_copies = []
    for place, owner in enumerate((opp_sib, opp, sib, t)):
        columns = pl.ds(pl.multiple_of(owner * block, block), block)
        copy = pltpu.make_async_copy(
            weight_hbm.at[:, columns], w_buf.at[place], w_sem.at[place]
        )
        copy.start()
        w_copies.append(copy)
    res_copy = pltpu.make_async_copy(residual_hbm, res_buf, res_sem)
    res_copy.start()

    def one_hot(j):
        pairs = patch_ref[j]
        row = (pairs[:, 0:1] - t * local_heads) * length + pairs[:, 1:2]
        spots = lax.broadcasted_iota(jnp.int32, (pairs.shape[0], local_heads * length), 1)
        return jnp.where(spots == row, 1.0, 0.0).astype(BF16)

    rows = local_heads * length
    s_id = lax.broadcasted_iota(jnp.int32, (length, rows), 0)
    i_id = lax.rem(lax.broadcasted_iota(jnp.int32, (length, rows), 1), length)
    causal = s_id <= i_id
    for j in range(prompts):
        q = jnp.concatenate(
            [q_ref[j, :, h * HDIM : (h + 1) * HDIM] for h in range(local_heads)], axis=0
        )
        scores = contract(k_ref[j], q, 1, 1) * (1.0 / math.sqrt(HDIM))
        scores = jnp.where(causal, scores, -jnp.inf)
        exponent = jnp.exp(scores - jnp.max(scores, axis=0, keepdims=True))
        weights = exponent * (1.0 / jnp.sum(exponent, axis=0, keepdims=True))
        heads = contract(weights.astype(BF16), v_ref[j], 0, 0).astype(BF16)
        heads_buf[j] = heads
        entry_send[j] = contract(one_hot(j), heads, 1, 0).astype(BF16)

    pl.semaphore_wait(barrier, n_dp + 1)
    entry_copy = pltpu.make_async_remote_copy(
        src_ref=entry_send,
        dst_ref=entry_recv,
        send_sem=entry_sem.at[0],
        recv_sem=entry_sem.at[1],
        device_id=(partner, t),
        device_id_type=MESH,
    )
    entry_copy.start()

    probe = probe_ref[...].astype(BF16)
    probe_buf[...] = jnp.concatenate([probe, jnp.zeros_like(probe)], axis=1)
    for j in range(prompts):
        class_id = lax.broadcasted_iota(jnp.int32, (classes, length), 0)
        target = jnp.where(class_id == label_ref[j : j + 1, :], 1.0, 0.0)
        target_buf[j] = target.T
    entry_copy.wait()

    for j in range(prompts):
        arrived = entry_recv[slot_ref[j]]
        both = jnp.concatenate([arrived, jnp.ones_like(arrived)], axis=1)
        placed = contract(one_hot(j), both, 0, 0)
        patched = jnp.where(
            placed[:, HDIM:] > 0.5, placed[:, :HDIM], heads_buf[j].astype(F32)
        ).astype(BF16)
        for h in range(local_heads):
            x_buf[j, :, h * HDIM : (h + 1) * HDIM] = patched[h * length : (h + 1) * length]

    def remote(source, target, sems, j, device):
        return pltpu.make_async_remote_copy(
            src_ref=source.at[j],
            dst_ref=target.at[j],
            send_sem=sems.at[0, j],
            recv_sem=sems.at[1, j],
            device_id=(d, device),
            device_id_type=MESH,
        )

    def project(j, place):
        return jnp.dot(x_buf[j], w_buf[place], preferred_element_type=F32).astype(BF16)

    def start_a(j):
        a_send[j] = project(j, 0)
        remote(a_send, a_recv, a_sems, j, sib).start()

    def start_c(j):
        mine = project(j, 1).astype(F32)
        remote(a_send, a_recv, a_sems, j, sib).wait()
        c_send[j] = (mine + a_recv[j].astype(F32)).astype(BF16)
        remote(c_send, c_recv, c_sems, j, opp).start()

    w_copies[0].wait()
    start_a(0)
    w_copies[1].wait()

    def first(j, carry):
        start_a(j + 1)
        start_c(j)
        return carry

    lax.fori_loop(0, prompts - 1, first, 0)
    start_c(prompts - 1)
    w_copies[2].wait()
    w_copies[3].wait()

    def second(j, carry):
        d_send[j] = project(j, 2)
        remote(d_send, d_recv, d_sems, j, sib).start()
        own_buf[j] = project(j, 3)
        return carry

    lax.fori_loop(0, prompts, second, 0)
    res_copy.wait()

    lane = lax.broadcasted_iota(jnp.int32, (length, LANES), 1)

    def pack(part, squares):
        high = squares.astype(BF16).astype(F32)
        part = jnp.where(lane == classes, high, part)
        part = jnp.where(lane == classes + 1, squares - high, part)
        return part.astype(BF16)

    def unpack(message):
        message = message.astype(F32)
        tail = jnp.where((lane == classes) | (lane == classes + 1), message, 0.0)
        return message, jnp.sum(tail, axis=1, keepdims=True)

    def out_copy(j):
        return pltpu.make_async_copy(out_buf.at[j], out_hbm.at[j], out_sem.at[j])

    def stage3(j):
        remote(d_send, d_recv, d_sems, j, sib).wait()
        remote(c_send, c_recv, c_sems, j, opp).wait()
        total = own_buf[j].astype(F32) + d_recv[j].astype(F32) + c_recv[j].astype(F32)
        attn = total.astype(BF16)
        out_buf[j] = attn
        out_copy(j).start()
        hidden = res_buf[j].astype(F32) + attn.astype(F32)
        squares = jnp.sum(hidden * hidden, axis=1, keepdims=True)
        hg = (hidden * gain_ref[...]).astype(BF16)
        hg_buf[pl.ds(pl.multiple_of(j * length, length), length), :] = hg
        part = jnp.dot(hg, probe_buf[...], preferred_element_type=F32)
        l1_send[j] = pack(part, squares)
        remote(l1_send, l1_recv, l1_sems, j, sib).start()

    def stage4(j):
        remote(l1_send, l1_recv, l1_sems, j, sib).wait()
        part_a, squares_a = unpack(l1_send[j])
        part_b, squares_b = unpack(l1_recv[j])
        l2_send[j] = pack(part_a + part_b, squares_a + squares_b)
        remote(l2_send, l2_recv, l2_sems, j, opp).start()

    def stage5(j):
        remote(l2_send, l2_recv, l2_sems, j, opp).wait()
        part_a, squares_a = unpack(l2_send[j])
        part_b, squares_b = unpack(l2_recv[j])
        inverse = lax.rsqrt((squares_a + squares_b) / width + norm_epsilon)
        logits = (part_a + part_b)[:, :classes] * inverse
        logits_ref[j] = logits
        error = jax.nn.sigmoid(logits) - target_buf[j]
        err_buf[pl.ds(pl.multiple_of(j * length, length), length), :] = (
            error * inverse
        ).astype(BF16)

    stage3(0)
    stage3(1)
    stage4(0)

    def third(j, carry):
        stage3(j)
        stage4(j - 1)
        stage5(j - 2)
        return carry

    lax.fori_loop(2, prompts, third, 0)
    last = prompts - 1
    stage5(last - 1)
    stage4(last)
    early = last * length
    grad = contract(err_buf[:early, :], hg_buf[:early, :], 0, 0)
    stage5(last)
    grad = grad + contract(err_buf[early:, :], hg_buf[early:, :], 0, 0)

    piece_rows = g_send.shape[1]
    per_column = classes // piece_rows
    for i in range(n_dp):
        column, row = i // per_column * LANES, i % per_column * piece_rows
        g_send[i] = grad[row : row + piece_rows, column : column + LANES].astype(g_send.dtype)

    def scatter(peer_to, peer_from):
        return pltpu.make_async_remote_copy(
            src_ref=g_send.at[peer_to],
            dst_ref=g_recv.at[peer_from],
            send_sem=rs_ssem.at[peer_to],
            recv_sem=rs_rsem.at[peer_from],
            device_id=(peer_to, t),
            device_id_type=MESH,
        )

    def gather(peer_to, piece):
        return pltpu.make_async_remote_copy(
            src_ref=ag_buf.at[piece],
            dst_ref=ag_buf.at[piece],
            send_sem=ag_ssem.at[peer_to],
            recv_sem=ag_rsem.at[piece],
            device_id=(peer_to, t),
            device_id_type=MESH,
        )

    peers = [lax.rem(d + off, n_dp) for off in range(1, n_dp)]
    for peer in peers:
        scatter(peer, d).start()
    g_recv[d] = g_send[d]
    for peer in peers:
        scatter(peer, peer).wait_recv()
    total = g_recv[0].astype(F32)
    for i in range(1, n_dp):
        total = total + g_recv[i].astype(F32)
    tokens = prompts * length * n_dp
    ag_buf[d] = (total * (1.0 / math.sqrt(tokens))).astype(ag_buf.dtype)
    for peer in peers:
        gather(peer, d).start()
    for peer in peers:
        gather(peer, peer).wait_recv()
    for column in range(features // LANES):
        piece = jnp.concatenate(
            [ag_buf[column * per_column + i].astype(F32) for i in range(per_column)], axis=0
        )
        grad_ref[column * LANES : (column + 1) * LANES, :] = piece.T
    for peer in peers:
        scatter(peer, peer).wait_send()
        gather(peer, d).wait_send()

    def finish(j, carry):
        out_copy(j).wait()
        return carry

    lax.fori_loop(0, prompts, finish, 0)


def per_device(
    residual,
    queries,
    attn_keys,
    values,
    out_weight,
    norm_gain,
    probe_weight,
    partner_slot,
    patch_list,
    concept_labels,
):
    n_dp = lax.axis_size("dp")
    prompts, length, block = residual.shape
    width = out_weight.shape[1]
    features = queries.shape[2]
    classes = probe_weight.shape[1]
    entries = patch_list.shape[1]
    rows = features // HDIM * length
    tokens = prompts * length
    piece_rows = classes * block // LANES // n_dp
    piece_type = BF16 if piece_rows % 16 == 0 else F32
    vmem = pl.BlockSpec(memory_space=pltpu.VMEM)
    smem = pl.BlockSpec(memory_space=pltpu.SMEM)
    anywhere = pl.BlockSpec(memory_space=pl.ANY)
    dma = pltpu.SemaphoreType.DMA
    part = pltpu.VMEM((prompts, length, block), BF16)
    message = pltpu.VMEM((prompts, length, LANES), BF16)
    pieces = pltpu.VMEM((n_dp, piece_rows, LANES), piece_type)
    scratch = [
        pltpu.VMEM((4, features, block), BF16),
        part,
        part,
        pltpu.VMEM((prompts, rows, HDIM), BF16),
        pltpu.VMEM((prompts, length, features), BF16),
        pltpu.VMEM((prompts, entries, HDIM), BF16),
        pltpu.VMEM((prompts, entries, HDIM), BF16),
        part,
        part,
        part,
        part,
        part,
        part,
        part,
        pltpu.VMEM((tokens, block), BF16),
        pltpu.VMEM((block, 2 * classes), BF16),
        pltpu.VMEM((prompts, length, classes), F32),
        pltpu.VMEM((tokens, classes), BF16),
        message,
        message,
        message,
        message,
        pieces,
        pieces,
        pieces,
        dma((4,)),
        dma,
        dma((prompts,)),
        dma((2,)),
        dma((2, prompts)),
        dma((2, prompts)),
        dma((2, prompts)),
        dma((2, prompts)),
        dma((2, prompts)),
        dma((n_dp,)),
        dma((n_dp,)),
        dma((n_dp,)),
        dma((n_dp,)),
    ]
    return pl.pallas_call(
        functools.partial(kernel, n_dp, width),
        out_shape=(
            jax.ShapeDtypeStruct((prompts, length, block), BF16),
            jax.ShapeDtypeStruct((prompts, length, classes), F32),
            jax.ShapeDtypeStruct((block, classes), F32),
        ),
        in_specs=[smem, vmem, vmem, vmem, vmem, vmem, vmem, vmem, anywhere, anywhere],
        out_specs=(anywhere, vmem, vmem),
        scratch_shapes=scratch,
        compiler_params=pltpu.CompilerParams(
            collective_id=0, has_side_effects=True, vmem_limit_bytes=48 * 1024 * 1024
        ),
    )(
        partner_slot,
        queries,
        attn_keys,
        values,
        patch_list,
        concept_labels,
        norm_gain.reshape(1, block),
        probe_weight,
        out_weight,
        residual,
    )


def solution(mesh):
    return jax.shard_map(
        per_device,
        mesh=mesh,
        in_specs=(
            P("dp", None, "tensor"),
            P("dp", None, "tensor"),
            P("dp", None, "tensor"),
            P("dp", None, "tensor"),
            P("tensor", None),
            P("tensor"),
            P("tensor", None),
            P("dp"),
            P("dp", "tensor", None),
            P("dp", None),
        ),
        out_specs=(P("dp", None, "tensor"), P("dp", None, None), P("tensor", None)),
        check_vma=False,
    )
```

```python
import functools
import math

import jax
import jax.numpy as jnp
from jax import lax
from jax.experimental import pallas as pl
from jax.experimental.pallas import tpu as pltpu
from jax.sharding import PartitionSpec as P

HDIM = 128
LANES = 128
norm_epsilon = 1e-05
MESH = pl.DeviceIdType.MESH
F32 = jnp.float32
BF16 = jnp.bfloat16


def contract(a, b, dim_a, dim_b):
    return lax.dot_general(
        a, b, (((dim_a,), (dim_b,)), ((), ())), preferred_element_type=F32
    )


def kernel(
    n_dp,
    width,
    length,
    slot_hbm,
    q_hbm,
    k_hbm,
    v_hbm,
    patch_hbm,
    label_hbm,
    gain_hbm,
    probe_hbm,
    weight_hbm,
    residual_hbm,
    out_hbm,
    logits_hbm,
    grad_hbm,
    slot_ref,
    q_ref,
    k_ref,
    v_ref,
    patch_ref,
    label_ref,
    gain_ref,
    probe_ref,
    w_buf,
    res_buf,
    out_buf,
    logits_ref,
    grad_ref,
    heads_buf,
    x_buf,
    entry_send,
    entry_recv,
    a_send,
    a_recv,
    c_send,
    c_recv,
    d_send,
    d_recv,
    own_buf,
    hg_buf,
    probe_buf,
    target_buf,
    err_buf,
    l1_send,
    l1_recv,
    l2_send,
    l2_recv,
    g_send,
    g_recv,
    ag_buf,
    in_sem,
    w_sem,
    out_sem,
    logits_sem,
    entry_sem,
    a_sems,
    c_sems,
    d_sems,
    l1_sems,
    l2_sems,
    rs_ssem,
    rs_rsem,
    ag_ssem,
    ag_rsem,
):
    prompts = k_ref.shape[0]
    tokens, features = q_ref.shape
    local_heads = features // HDIM
    classes = probe_ref.shape[0]
    block = res_buf.shape[1]
    d = lax.axis_index("dp")
    t = lax.axis_index("tensor")
    core = lax.rem(t, 2)
    sib = t + 1 - 2 * core
    opp = lax.rem(t + 2, 4)
    opp_sib = lax.rem(sib + 2, 4)
    partner = lax.rem(d + n_dp // 2, n_dp)

    barrier = pltpu.get_barrier_semaphore()
    pl.semaphore_signal(barrier, inc=1, device_id=(d, sib), device_id_type=MESH)
    pl.semaphore_signal(barrier, inc=1, device_id=(d, opp), device_id_type=MESH)
    for off in range(1, n_dp):
        pl.semaphore_signal(
            barrier, inc=1, device_id=(lax.rem(d + off, n_dp), t), device_id_type=MESH
        )

    in_copies = []
    for place, (source, target) in enumerate(
        (
            (patch_hbm, patch_ref),
            (q_hbm, q_ref),
            (k_hbm, k_ref),
            (v_hbm, v_ref),
            (slot_hbm, slot_ref),
            (label_hbm, label_ref),
            (probe_hbm, probe_ref),
            (gain_hbm, gain_ref),
            (residual_hbm, res_buf),
        )
    ):
        copy = pltpu.make_async_copy(source, target, in_sem.at[place])
        in_copies.append(copy)
    w_copies = []
    for place, owner in enumerate((opp_sib, opp, sib, t)):
        columns = pl.ds(pl.multiple_of(owner * block, block), block)
        copy = pltpu.make_async_copy(
            weight_hbm.at[:, columns], w_buf.at[place], w_sem.at[place]
        )
        w_copies.append(copy)
    for copy in in_copies[:8] + w_copies + in_copies[8:]:
        copy.start()

    rows = local_heads * length
    spots = lax.broadcasted_iota(jnp.int32, (rows, patch_ref.shape[2]), 0)

    def one_hot(j):
        pairs = patch_ref[j]
        row = (pairs[0:1, :] - t * local_heads) * length + pairs[1:2, :]
        return jnp.where(spots == row, 1.0, 0.0).astype(BF16)

    def queries_of(j):
        low = j * length
        return jnp.concatenate(
            [
                q_ref[low : low + length, h * HDIM : (h + 1) * HDIM]
                for h in range(local_heads)
            ],
            axis=0,
        )

    def weights_of(scores, causal):
        scores = jnp.where(causal, scores * (1.0 / math.sqrt(HDIM)), -jnp.inf)
        exponent = jnp.exp(scores - jnp.max(scores, axis=0, keepdims=True))
        total = jnp.sum(exponent, axis=0, keepdims=True)
        return (exponent * (1.0 / total)).astype(BF16)

    every = range(prompts)
    for copy in in_copies[:4]:
        copy.wait()
    picked = [contract(one_hot(j), queries_of(j), 0, 0).astype(BF16) for j in every]
    scores = [contract(k_ref[j], picked[j], 1, 1) for j in every]
    s_id = lax.broadcasted_iota(jnp.int32, scores[0].shape, 0)
    weights = [weights_of(scores[j], s_id <= patch_ref[j][1:2, :]) for j in every]
    for j in every:
        entry_send[j] = contract(weights[j], v_ref[j], 0, 0).astype(BF16)

    pl.semaphore_wait(barrier, n_dp + 1)
    entry_copy = pltpu.make_async_remote_copy(
        src_ref=entry_send,
        dst_ref=entry_recv,
        send_sem=entry_sem.at[0],
        recv_sem=entry_sem.at[1],
        device_id=(partner, t),
        device_id_type=MESH,
    )
    entry_copy.start()

    s_id = lax.broadcasted_iota(jnp.int32, (length, rows), 0)
    i_id = lax.rem(lax.broadcasted_iota(jnp.int32, (length, rows), 1), length)
    causal = s_id <= i_id
    for low in range(0, prompts, 2):
        some = range(low, min(low + 2, prompts))
        scores = [contract(k_ref[j], queries_of(j), 1, 1) for j in some]
        weights = [weights_of(part, causal) for part in scores]
        for j, part in zip(some, weights):
            heads_buf[j] = contract(part, v_ref[j], 0, 0).astype(BF16)

    for copy in in_copies[4:8]:
        copy.wait()
    probe = probe_ref[...].astype(BF16)
    probe_buf[...] = jnp.concatenate([probe, jnp.zeros_like(probe)], axis=0)
    for j in every:
        class_id = lax.broadcasted_iota(jnp.int32, (classes, length), 0)
        target = jnp.where(class_id == label_ref[j : j + 1, :], 1.0, 0.0)
        target_buf[j] = target.T
    entry_copy.wait()

    def patch(j):
        arrived = entry_recv[slot_ref[j]]
        both = jnp.concatenate([arrived, jnp.ones_like(arrived)], axis=1)
        placed = contract(one_hot(j), both, 1, 0)
        patched = jnp.where(
            placed[:, HDIM:] > 0.5, placed[:, :HDIM], heads_buf[j].astype(F32)
        ).astype(BF16)
        for h in range(local_heads):
            x_buf[chunk(j), h * HDIM : (h + 1) * HDIM] = patched[
                h * length : (h + 1) * length
            ]

    def chunk(j):
        return pl.ds(pl.multiple_of(j * length, length), length)

    def remote(source, target, sems, j, device, place=None):
        place = chunk(j) if place is None else place
        return pltpu.make_async_remote_copy(
            src_ref=source.at[place],
            dst_ref=target.at[place],
            send_sem=sems.at[0, j],
            recv_sem=sems.at[1, j],
            device_id=(d, device),
            device_id_type=MESH,
        )

    def project(rows, place):
        return jnp.dot(x_buf[rows, :], w_buf[place], preferred_element_type=F32).astype(BF16)

    def start_a(j):
        a_send[chunk(j), :] = project(chunk(j), 0)
        remote(a_send, a_recv, a_sems, j, sib).start()

    def start_c(j):
        mine = project(chunk(j), 1).astype(F32)
        remote(a_send, a_recv, a_sems, j, sib).wait()
        c_send[chunk(j), :] = (mine + a_recv[chunk(j), :].astype(F32)).astype(BF16)
        remote(c_send, c_recv, c_sems, j, opp).start()

    patch(0)
    w_copies[0].wait()
    start_a(0)
    w_copies[1].wait()

    def first(j, carry):
        patch(j + 1)
        start_a(j + 1)
        start_c(j)
        return carry

    lax.fori_loop(0, prompts - 1, first, 0)
    start_c(prompts - 1)
    w_copies[2].wait()
    w_copies[3].wait()
    halves = d_sems.shape[1]
    half = tokens // halves

    def d_copy(j):
        place = pl.ds(pl.multiple_of(j * half, half), half)
        return remote(d_send, d_recv, d_sems, j, sib, place)

    def second(j, carry):
        place = pl.ds(pl.multiple_of(j * half, half), half)
        d_send[place, :] = project(place, 2)
        d_copy(j).start()
        own_buf[place, :] = project(place, 3)
        return carry

    lax.fori_loop(0, halves, second, 0)
    in_copies[8].wait()
    for j in range(halves):
        d_copy(j).wait()

    lane = lax.broadcasted_iota(jnp.int32, (length, LANES), 1)

    def pack(part, squares):
        high = squares.astype(BF16).astype(F32)
        part = jnp.where(lane == classes, high, part)
        part = jnp.where(lane == classes + 1, squares - high, part)
        return part.astype(BF16)

    def unpack(message):
        message = message.astype(F32)
        tail = jnp.where((lane == classes) | (lane == classes + 1), message, 0.0)
        return message, jnp.sum(tail, axis=1, keepdims=True)

    def out_copy(j):
        return pltpu.make_async_copy(
            out_buf.at[chunk(j)], out_hbm.at[chunk(j)], out_sem.at[j]
        )

    def logits_copy(j):
        return pltpu.make_async_copy(logits_ref.at[j], logits_hbm.at[j], logits_sem.at[j])

    def stage3(j):
        remote(c_send, c_recv, c_sems, j, opp).wait()
        at = chunk(j)
        own = own_buf[at, :].astype(F32) + d_recv[at, :].astype(F32)
        attn = (own + c_recv[at, :].astype(F32)).astype(BF16)
        out_buf[at, :] = attn
        out_copy(j).start()
        hidden = res_buf[at, :].astype(F32) + attn.astype(F32)
        squares = jnp.sum(hidden * hidden, axis=1, keepdims=True)
        hg = (hidden * gain_ref[...]).astype(BF16)
        hg_buf[at, :] = hg
        part = contract(hg, probe_buf[...], 1, 1)
        l1_send[j] = pack(part, squares)
        remote(l1_send, l1_recv, l1_sems, j, sib, j).start()

    def stage4(j):
        remote(l1_send, l1_recv, l1_sems, j, sib, j).wait()
        part_a, squares_a = unpack(l1_send[j])
        part_b, squares_b = unpack(l1_recv[j])
        l2_send[j] = pack(part_a + part_b, squares_a + squares_b)
        remote(l2_send, l2_recv, l2_sems, j, opp, j).start()

    def stage5(j):
        remote(l2_send, l2_recv, l2_sems, j, opp, j).wait()
        part_a, squares_a = unpack(l2_send[j])
        part_b, squares_b = unpack(l2_recv[j])
        inverse = lax.rsqrt((squares_a + squares_b) / width + norm_epsilon)
        logits = (part_a + part_b)[:, :classes] * inverse
        logits_ref[j] = logits
        logits_copy(j).start()
        error = jax.nn.sigmoid(logits) - target_buf[j]
        err_buf[chunk(j), :] = (error * inverse).astype(BF16)

    stage3(0)
    stage3(1)
    stage4(0)

    def third(j, carry):
        stage3(j)
        stage4(j - 1)
        stage5(j - 2)
        return carry

    lax.fori_loop(2, prompts, third, 0)
    last = prompts - 1
    stage5(last - 1)
    stage4(last)
    early = last * length
    grad = contract(err_buf[:early, :], hg_buf[:early, :], 0, 0)
    stage5(last)
    grad = grad + contract(err_buf[early:, :], hg_buf[early:, :], 0, 0)

    piece_rows = g_send.shape[1]
    per_column = classes // piece_rows
    for i in range(n_dp):
        column, row = i // per_column * LANES, i % per_column * piece_rows
        g_send[i] = grad[row : row + piece_rows, column : column + LANES].astype(g_send.dtype)

    def scatter(peer_to, peer_from):
        return pltpu.make_async_remote_copy(
            src_ref=g_send.at[peer_to],
            dst_ref=g_recv.at[peer_from],
            send_sem=rs_ssem.at[peer_to],
            recv_sem=rs_rsem.at[peer_from],
            device_id=(peer_to, t),
            device_id_type=MESH,
        )

    def gather(peer_to, piece):
        return pltpu.make_async_remote_copy(
            src_ref=ag_buf.at[piece],
            dst_ref=ag_buf.at[piece],
            send_sem=ag_ssem.at[peer_to],
            recv_sem=ag_rsem.at[piece],
            device_id=(peer_to, t),
            device_id_type=MESH,
        )

    peers = [lax.rem(d + off, n_dp) for off in range(1, n_dp)]
    for peer in peers:
        scatter(peer, d).start()
    g_recv[d] = g_send[d]
    for peer in peers:
        scatter(peer, peer).wait_recv()
    total = g_recv[0].astype(F32)
    for i in range(1, n_dp):
        total = total + g_recv[i].astype(F32)
    ag_buf[d] = (total * (1.0 / math.sqrt(tokens * n_dp))).astype(ag_buf.dtype)
    for peer in peers:
        gather(peer, d).start()
    for peer in peers:
        gather(peer, peer).wait_recv()
    for i in range(n_dp):
        column, row = i // per_column * LANES, i % per_column * piece_rows
        grad_ref[row : row + piece_rows, column : column + LANES] = ag_buf[i].astype(F32)
    grad_copy = pltpu.make_async_copy(grad_ref, grad_hbm, in_sem.at[0])
    grad_copy.start()
    for peer in peers:
        scatter(peer, peer).wait_send()
        gather(peer, d).wait_send()

    def finish(j, carry):
        out_copy(j).wait()
        logits_copy(j).wait()
        return carry

    lax.fori_loop(0, prompts, finish, 0)
    grad_copy.wait()


def per_device(
    residual,
    queries,
    attn_keys,
    values,
    out_weight,
    norm_gain,
    probe_weight,
    partner_slot,
    patch_list,
    concept_labels,
):
    n_dp = lax.axis_size("dp")
    prompts, length, block = residual.shape
    width = out_weight.shape[1]
    features = queries.shape[2]
    classes = probe_weight.shape[1]
    entries = patch_list.shape[1]
    rows = features // HDIM * length
    tokens = prompts * length
    piece_rows = classes * block // LANES // n_dp
    piece_type = BF16 if piece_rows % 16 == 0 else F32
    anywhere = pl.BlockSpec(memory_space=pl.ANY)
    dma = pltpu.SemaphoreType.DMA
    part = pltpu.VMEM((tokens, block), BF16)
    message = pltpu.VMEM((prompts, length, LANES), BF16)
    pieces = pltpu.VMEM((n_dp, piece_rows, LANES), piece_type)
    scratch = [
        pltpu.SMEM((prompts,), jnp.int32),
        pltpu.VMEM((tokens, features), BF16),
        pltpu.VMEM(attn_keys.shape, BF16),
        pltpu.VMEM(values.shape, BF16),
        pltpu.VMEM((prompts, 2, entries), jnp.int32),
        pltpu.VMEM(concept_labels.shape, jnp.int32),
        pltpu.VMEM((1, block), F32),
        pltpu.VMEM((classes, block), F32),
        pltpu.VMEM((4, features, block), BF16),
        part,
        part,
        pltpu.VMEM((prompts, length, classes), F32),
        pltpu.VMEM((classes, block), F32),
        pltpu.VMEM((prompts, rows, HDIM), BF16),
        pltpu.VMEM((tokens, features), BF16),
        pltpu.VMEM((prompts, entries, HDIM), BF16),
        pltpu.VMEM((prompts, entries, HDIM), BF16),
        part,
        part,
        part,
        part,
        part,
        part,
        part,
        part,
        pltpu.VMEM((2 * classes, block), BF16),
        pltpu.VMEM((prompts, length, classes), F32),
        pltpu.VMEM((tokens, classes), BF16),
        message,
        message,
        message,
        message,
        pieces,
        pieces,
        pieces,
        dma((9,)),
        dma((4,)),
        dma((prompts,)),
        dma((prompts,)),
        dma((2,)),
        dma((2, prompts)),
        dma((2, prompts)),
        dma((2, 2)),
        dma((2, prompts)),
        dma((2, prompts)),
        dma((n_dp,)),
        dma((n_dp,)),
        dma((n_dp,)),
        dma((n_dp,)),
    ]
    attn_out, logits, grad = pl.pallas_call(
        functools.partial(kernel, n_dp, width, length),
        out_shape=(
            jax.ShapeDtypeStruct((tokens, block), BF16),
            jax.ShapeDtypeStruct((prompts, length, classes), F32),
            jax.ShapeDtypeStruct((classes, block), F32),
        ),
        in_specs=[anywhere] * 10,
        out_specs=(anywhere,) * 3,
        scratch_shapes=scratch,
        compiler_params=pltpu.CompilerParams(
            collective_id=0, has_side_effects=True, vmem_limit_bytes=60 * 1024 * 1024
        ),
    )(
        partner_slot,
        queries.reshape(tokens, features),
        attn_keys,
        values,
        jnp.swapaxes(patch_list, 1, 2),
        concept_labels,
        norm_gain.reshape(1, block),
        probe_weight.T,
        out_weight,
        residual.reshape(tokens, block),
    )
    return attn_out.reshape(prompts, length, block), logits, grad.T


def solution(mesh):
    return jax.shard_map(
        per_device,
        mesh=mesh,
        in_specs=(
            P("dp", None, "tensor"),
            P("dp", None, "tensor"),
            P("dp", None, "tensor"),
            P("dp", None, "tensor"),
            P("tensor", None),
            P("tensor"),
            P("tensor", None),
            P("dp"),
            P("dp", "tensor", None),
            P("dp", None),
        ),
        out_specs=(P("dp", None, "tensor"), P("dp", None, None), P("tensor", None)),
        check_vma=False,
    )
```

```python
import functools
import math

import jax
import jax.numpy as jnp
from jax import lax
from jax.experimental import pallas as pl
from jax.experimental.pallas import tpu as pltpu
from jax.sharding import PartitionSpec as P

HDIM = 128
LANES = 128
VMEM_BYTES = 62 * 1024 * 1024
norm_epsilon = 1e-05
MESH = pl.DeviceIdType.MESH
F32 = jnp.float32
BF16 = jnp.bfloat16


def contract(a, b, dim_a, dim_b):
    return lax.dot_general(
        a, b, (((dim_a,), (dim_b,)), ((), ())), preferred_element_type=F32
    )


def kernel(
    n_dp,
    width,
    length,
    slot_hbm,
    q_hbm,
    k_hbm,
    v_hbm,
    patch_hbm,
    label_hbm,
    gain_hbm,
    probe_hbm,
    weight_hbm,
    residual_hbm,
    out_hbm,
    logits_hbm,
    grad_hbm,
    slot_ref,
    q_ref,
    k_ref,
    v_ref,
    patch_ref,
    label_ref,
    gain_ref,
    probe_ref,
    w_buf,
    res_buf,
    out_buf,
    logits_ref,
    grad_ref,
    heads_buf,
    x_buf,
    entry_send,
    entry_recv,
    a_send,
    a_recv,
    c_send,
    c_recv,
    d_send,
    d_recv,
    own_buf,
    hg_buf,
    probe_buf,
    target_buf,
    err_buf,
    l1_send,
    l1_recv,
    l2_send,
    l2_recv,
    g_send,
    g_recv,
    ag_buf,
    in_sem,
    w_sem,
    out_sem,
    entry_sem,
    a_sems,
    c_sems,
    d_sems,
    l1_sems,
    l2_sems,
    rs_ssem,
    rs_rsem,
    ag_ssem,
    ag_rsem,
):
    prompts = k_ref.shape[0]
    tokens, features = q_ref.shape
    local_heads = features // HDIM
    classes = probe_ref.shape[0]
    block = res_buf.shape[1]
    d = lax.axis_index("dp")
    t = lax.axis_index("tensor")
    core = lax.rem(t, 2)
    sib = t + 1 - 2 * core
    opp = lax.rem(t + 2, 4)
    opp_sib = lax.rem(sib + 2, 4)
    partner = lax.rem(d + n_dp // 2, n_dp)

    barrier = pltpu.get_barrier_semaphore()
    pl.semaphore_signal(barrier, inc=1, device_id=(d, sib), device_id_type=MESH)
    pl.semaphore_signal(barrier, inc=1, device_id=(d, opp), device_id_type=MESH)
    for off in range(1, n_dp):
        pl.semaphore_signal(
            barrier, inc=1, device_id=(lax.rem(d + off, n_dp), t), device_id_type=MESH
        )

    in_copies = []
    for place, (source, target) in enumerate(
        (
            (patch_hbm, patch_ref),
            (q_hbm, q_ref),
            (k_hbm, k_ref),
            (v_hbm, v_ref),
            (slot_hbm, slot_ref),
            (label_hbm, label_ref),
            (probe_hbm, probe_ref),
            (gain_hbm, gain_ref),
            (residual_hbm, res_buf),
        )
    ):
        copy = pltpu.make_async_copy(source, target, in_sem.at[place])
        in_copies.append(copy)
    w_copies = []
    for place, owner in enumerate((opp_sib, opp, sib, t)):
        columns = pl.ds(pl.multiple_of(owner * block, block), block)
        copy = pltpu.make_async_copy(
            weight_hbm.at[:, columns], w_buf.at[place], w_sem.at[place]
        )
        w_copies.append(copy)
    for copy in in_copies[:8] + w_copies + in_copies[8:]:
        copy.start()

    rows = local_heads * length
    spots = lax.broadcasted_iota(jnp.int32, (rows, patch_ref.shape[2]), 0)

    def one_hot(j):
        pairs = patch_ref[j]
        row = (pairs[0:1, :] - t * local_heads) * length + pairs[1:2, :]
        return jnp.where(spots == row, 1.0, 0.0).astype(BF16)

    def queries_of(j):
        low = j * length
        return jnp.concatenate(
            [
                q_ref[low : low + length, h * HDIM : (h + 1) * HDIM]
                for h in range(local_heads)
            ],
            axis=0,
        )

    def weights_of(scores, causal):
        scores = jnp.where(causal, scores * (1.0 / math.sqrt(HDIM)), -jnp.inf)
        exponent = jnp.exp(scores - jnp.max(scores, axis=0, keepdims=True))
        total = jnp.sum(exponent, axis=0, keepdims=True)
        return (exponent * (1.0 / total)).astype(BF16)

    every = range(prompts)
    for copy in in_copies[:4]:
        copy.wait()
    picked = [contract(one_hot(j), queries_of(j), 0, 0).astype(BF16) for j in every]
    scores = [contract(k_ref[j], picked[j], 1, 1) for j in every]
    s_id = lax.broadcasted_iota(jnp.int32, scores[0].shape, 0)
    weights = [weights_of(scores[j], s_id <= patch_ref[j][1:2, :]) for j in every]
    for j in every:
        entry_send[j] = contract(weights[j], v_ref[j], 0, 0).astype(BF16)

    pl.semaphore_wait(barrier, n_dp + 1)
    entry_copy = pltpu.make_async_remote_copy(
        src_ref=entry_send,
        dst_ref=entry_recv,
        send_sem=entry_sem.at[0],
        recv_sem=entry_sem.at[1],
        device_id=(partner, t),
        device_id_type=MESH,
    )
    entry_copy.start()

    s_id = lax.broadcasted_iota(jnp.int32, (length, rows), 0)
    i_id = lax.rem(lax.broadcasted_iota(jnp.int32, (length, rows), 1), length)
    causal = s_id <= i_id
    for low in range(0, prompts, 2):
        some = range(low, min(low + 2, prompts))
        scores = [contract(k_ref[j], queries_of(j), 1, 1) for j in some]
        weights = [weights_of(part, causal) for part in scores]
        for j, part in zip(some, weights):
            heads_buf[j] = contract(part, v_ref[j], 0, 0).astype(BF16)

    for copy in in_copies[4:8]:
        copy.wait()
    probe = probe_ref[...].astype(BF16)
    probe_buf[...] = jnp.concatenate([probe, jnp.zeros_like(probe)], axis=0)
    for j in every:
        class_id = lax.broadcasted_iota(jnp.int32, (classes, length), 0)
        target = jnp.where(class_id == label_ref[j : j + 1, :], 1.0, 0.0)
        target_buf[j] = target.T
    entry_copy.wait()

    def patch(j):
        arrived = entry_recv[slot_ref[j]]
        both = jnp.concatenate([arrived, jnp.ones_like(arrived)], axis=1)
        placed = contract(one_hot(j), both, 1, 0)
        patched = jnp.where(
            placed[:, HDIM:] > 0.5, placed[:, :HDIM], heads_buf[j].astype(F32)
        ).astype(BF16)
        for h in range(local_heads):
            x_buf[chunk(j), h * HDIM : (h + 1) * HDIM] = patched[
                h * length : (h + 1) * length
            ]

    def chunk(j):
        return pl.ds(pl.multiple_of(j * length, length), length)

    def remote(source, target, sems, j, device, place=None):
        place = chunk(j) if place is None else place
        return pltpu.make_async_remote_copy(
            src_ref=source.at[place],
            dst_ref=target.at[place],
            send_sem=sems.at[0, j],
            recv_sem=sems.at[1, j],
            device_id=(d, device),
            device_id_type=MESH,
        )

    def project(rows, place):
        return jnp.dot(x_buf[rows, :], w_buf[place], preferred_element_type=F32).astype(BF16)

    def start_a(j):
        a_send[chunk(j), :] = project(chunk(j), 0)
        remote(a_send, a_recv, a_sems, j, sib).start()

    def start_c(j):
        mine = project(chunk(j), 1).astype(F32)
        remote(a_send, a_recv, a_sems, j, sib).wait()
        c_send[chunk(j), :] = (mine + a_recv[chunk(j), :].astype(F32)).astype(BF16)
        remote(c_send, c_recv, c_sems, j, opp).start()

    patch(0)
    w_copies[0].wait()
    start_a(0)
    w_copies[1].wait()

    def first(j, carry):
        patch(j + 1)
        start_a(j + 1)
        start_c(j)
        return carry

    lax.fori_loop(0, prompts - 1, first, 0)
    start_c(prompts - 1)
    w_copies[2].wait()
    w_copies[3].wait()
    halves = d_sems.shape[1]
    half = tokens // halves

    def d_copy(j):
        place = pl.ds(pl.multiple_of(j * half, half), half)
        return remote(d_send, d_recv, d_sems, j, sib, place)

    def second(j, carry):
        place = pl.ds(pl.multiple_of(j * half, half), half)
        d_send[place, :] = project(place, 2)
        d_copy(j).start()
        own_buf[place, :] = project(place, 3)
        return carry

    lax.fori_loop(0, halves, second, 0)
    in_copies[8].wait()
    for j in range(halves):
        d_copy(j).wait()

    lane = lax.broadcasted_iota(jnp.int32, (length, LANES), 1)

    def pack(part, squares):
        high = squares.astype(BF16).astype(F32)
        part = jnp.where(lane == classes, high, part)
        part = jnp.where(lane == classes + 1, squares - high, part)
        return part.astype(BF16)

    def unpack(message):
        message = message.astype(F32)
        tail = jnp.where((lane == classes) | (lane == classes + 1), message, 0.0)
        return message, jnp.sum(tail, axis=1, keepdims=True)

    def stage3(j):
        remote(c_send, c_recv, c_sems, j, opp).wait()
        at = chunk(j)
        own = own_buf[at, :].astype(F32) + d_recv[at, :].astype(F32)
        attn = (own + c_recv[at, :].astype(F32)).astype(BF16)
        out_buf[at, :] = attn
        hidden = res_buf[at, :].astype(F32) + attn.astype(F32)
        squares = jnp.sum(hidden * hidden, axis=1, keepdims=True)
        hg = (hidden * gain_ref[...]).astype(BF16)
        hg_buf[at, :] = hg
        part = contract(hg, probe_buf[...], 1, 1)
        l1_send[j] = pack(part, squares)
        remote(l1_send, l1_recv, l1_sems, j, sib, j).start()

    def stage4(j):
        remote(l1_send, l1_recv, l1_sems, j, sib, j).wait()
        part_a, squares_a = unpack(l1_send[j])
        part_b, squares_b = unpack(l1_recv[j])
        l2_send[j] = pack(part_a + part_b, squares_a + squares_b)
        remote(l2_send, l2_recv, l2_sems, j, opp, j).start()

    def stage5(j):
        remote(l2_send, l2_recv, l2_sems, j, opp, j).wait()
        part_a, squares_a = unpack(l2_send[j])
        part_b, squares_b = unpack(l2_recv[j])
        inverse = lax.rsqrt((squares_a + squares_b) / width + norm_epsilon)
        logits = (part_a + part_b)[:, :classes] * inverse
        logits_ref[j] = logits
        error = jax.nn.sigmoid(logits) - target_buf[j]
        err_buf[chunk(j), :] = (error * inverse).astype(BF16)

    out_copies = [
        pltpu.make_async_copy(source, target, out_sem.at[place])
        for place, (source, target) in enumerate(
            ((out_buf, out_hbm), (logits_ref, logits_hbm), (grad_ref, grad_hbm))
        )
    ]
    stage3(0)

    def third(j, carry):
        stage3(j)
        stage4(j - 1)
        return carry

    def fourth(j, carry):
        stage5(j)
        return carry

    lax.fori_loop(1, prompts, third, 0)
    out_copies[0].start()
    last = prompts - 1
    stage4(last)
    lax.fori_loop(0, last, fourth, 0)
    early = last * length
    grad = contract(err_buf[:early, :], hg_buf[:early, :], 0, 0)
    stage5(last)
    out_copies[1].start()
    grad = grad + contract(err_buf[early:, :], hg_buf[early:, :], 0, 0)

    piece_rows = g_send.shape[1]
    per_column = classes // piece_rows
    for i in range(n_dp):
        column, row = i // per_column * LANES, i % per_column * piece_rows
        g_send[i] = grad[row : row + piece_rows, column : column + LANES].astype(g_send.dtype)

    def scatter(peer_to, peer_from):
        return pltpu.make_async_remote_copy(
            src_ref=g_send.at[peer_to],
            dst_ref=g_recv.at[peer_from],
            send_sem=rs_ssem.at[peer_to],
            recv_sem=rs_rsem.at[peer_from],
            device_id=(peer_to, t),
            device_id_type=MESH,
        )

    def gather(peer_to, piece):
        return pltpu.make_async_remote_copy(
            src_ref=ag_buf.at[piece],
            dst_ref=ag_buf.at[piece],
            send_sem=ag_ssem.at[peer_to],
            recv_sem=ag_rsem.at[piece],
            device_id=(peer_to, t),
            device_id_type=MESH,
        )

    peers = [lax.rem(d + off, n_dp) for off in range(1, n_dp)]
    for peer in peers:
        scatter(peer, d).start()
    g_recv[d] = g_send[d]
    for peer in peers:
        scatter(peer, peer).wait_recv()
    total = g_recv[0].astype(F32)
    for i in range(1, n_dp):
        total = total + g_recv[i].astype(F32)
    ag_buf[d] = (total * (1.0 / math.sqrt(tokens * n_dp))).astype(ag_buf.dtype)
    for peer in peers:
        gather(peer, d).start()
    for peer in peers:
        gather(peer, peer).wait_recv()
    for i in range(n_dp):
        column, row = i // per_column * LANES, i % per_column * piece_rows
        grad_ref[row : row + piece_rows, column : column + LANES] = ag_buf[i].astype(F32)
    out_copies[2].start()
    for peer in peers:
        scatter(peer, peer).wait_send()
        gather(peer, d).wait_send()
    for copy in out_copies:
        copy.wait()


def store_kernel(*refs):
    count = len(refs) // 2
    sems = refs[-1]
    copies = [
        pltpu.make_async_copy(refs[i], refs[count + i], sems.at[i]) for i in range(count)
    ]
    for copy in copies:
        copy.start()
    for copy in copies:
        copy.wait()


def per_device(
    residual,
    queries,
    attn_keys,
    values,
    out_weight,
    norm_gain,
    probe_weight,
    partner_slot,
    patch_list,
    concept_labels,
):
    n_dp = lax.axis_size("dp")
    prompts, length, block = residual.shape
    width = out_weight.shape[1]
    features = queries.shape[2]
    classes = probe_weight.shape[1]
    entries = patch_list.shape[1]
    rows = features // HDIM * length
    tokens = prompts * length
    piece_rows = classes * block // LANES // n_dp
    piece_type = BF16 if piece_rows % 16 == 0 else F32
    anywhere = pl.BlockSpec(memory_space=pl.ANY)
    dma = pltpu.SemaphoreType.DMA
    part = pltpu.VMEM((tokens, block), BF16)
    message = pltpu.VMEM((prompts, length, LANES), BF16)
    pieces = pltpu.VMEM((n_dp, piece_rows, LANES), piece_type)
    scratch = [
        pltpu.SMEM((prompts,), jnp.int32),
        pltpu.VMEM((tokens, features), BF16),
        pltpu.VMEM(attn_keys.shape, BF16),
        pltpu.VMEM(values.shape, BF16),
        pltpu.VMEM((prompts, 2, entries), jnp.int32),
        pltpu.VMEM(concept_labels.shape, jnp.int32),
        pltpu.VMEM((1, block), F32),
        pltpu.VMEM((classes, block), F32),
        pltpu.VMEM((4, features, block), BF16),
        part,
        part,
        pltpu.VMEM((prompts, length, classes), F32),
        pltpu.VMEM((classes, block), F32),
        pltpu.VMEM((prompts, rows, HDIM), BF16),
        pltpu.VMEM((tokens, features), BF16),
        pltpu.VMEM((prompts, entries, HDIM), BF16),
        pltpu.VMEM((prompts, entries, HDIM), BF16),
        part,
        part,
        part,
        part,
        part,
        part,
        part,
        part,
        pltpu.VMEM((2 * classes, block), BF16),
        pltpu.VMEM((prompts, length, classes), F32),
        pltpu.VMEM((tokens, classes), BF16),
        message,
        message,
        message,
        message,
        pieces,
        pieces,
        pieces,
        dma((9,)),
        dma((4,)),
        dma((3,)),
        dma((2,)),
        dma((2, prompts)),
        dma((2, prompts)),
        dma((2, 2)),
        dma((2, prompts)),
        dma((2, prompts)),
        dma((n_dp,)),
        dma((n_dp,)),
        dma((n_dp,)),
        dma((n_dp,)),
    ]
    results = (
        jax.ShapeDtypeStruct((tokens, block), BF16),
        jax.ShapeDtypeStruct((prompts, length, classes), F32),
        jax.ShapeDtypeStruct((classes, block), F32),
    )
    held = pl.pallas_call(
        functools.partial(kernel, n_dp, width, length),
        out_shape=results,
        in_specs=[anywhere] * 10,
        out_specs=(anywhere,) * 3,
        scratch_shapes=scratch,
        compiler_params=pltpu.CompilerParams(
            collective_id=0, has_side_effects=True, vmem_limit_bytes=VMEM_BYTES
        ),
    )(
        partner_slot,
        queries.reshape(tokens, features),
        attn_keys,
        values,
        jnp.swapaxes(patch_list, 1, 2),
        concept_labels,
        norm_gain.reshape(1, block),
        probe_weight.T,
        out_weight,
        residual.reshape(tokens, block),
    )
    attn_out, logits, grad = pl.pallas_call(
        store_kernel,
        out_shape=results,
        in_specs=[anywhere] * 3,
        out_specs=(anywhere,) * 3,
        scratch_shapes=[dma((3,))],
        compiler_params=pltpu.CompilerParams(vmem_limit_bytes=VMEM_BYTES),
    )(*held)
    return attn_out.reshape(prompts, length, block), logits, grad.T


def solution(mesh):
    return jax.shard_map(
        per_device,
        mesh=mesh,
        in_specs=(
            P("dp", None, "tensor"),
            P("dp", None, "tensor"),
            P("dp", None, "tensor"),
            P("dp", None, "tensor"),
            P("tensor", None),
            P("tensor"),
            P("tensor", None),
            P("dp"),
            P("dp", "tensor", None),
            P("dp", None),
        ),
        out_specs=(P("dp", None, "tensor"), P("dp", None, None), P("tensor", None)),
        check_vma=False,
    )
```

```python
import functools
import math

import jax
import jax.numpy as jnp
from jax import lax
from jax.experimental import pallas as pl
from jax.experimental.pallas import tpu as pltpu
from jax.sharding import PartitionSpec as P

HDIM = 128
LANES = 128
STORE_PARTS = 2
VMEM_BYTES = 62 * 1024 * 1024
norm_epsilon = 1e-05
MESH = pl.DeviceIdType.MESH
F32 = jnp.float32
BF16 = jnp.bfloat16


def contract(a, b, dim_a, dim_b):
    return lax.dot_general(
        a, b, (((dim_a,), (dim_b,)), ((), ())), preferred_element_type=F32
    )


def kernel(
    n_dp,
    width,
    length,
    slot_hbm,
    q_hbm,
    k_hbm,
    v_hbm,
    patch_hbm,
    label_hbm,
    gain_hbm,
    probe_hbm,
    weight_hbm,
    residual_hbm,
    out_hbm,
    logits_hbm,
    grad_hbm,
    slot_ref,
    q_ref,
    k_ref,
    v_ref,
    patch_ref,
    label_ref,
    gain_ref,
    probe_ref,
    w_buf,
    res_buf,
    out_buf,
    logits_ref,
    grad_ref,
    heads_buf,
    x_buf,
    entry_send,
    entry_recv,
    a_send,
    a_recv,
    c_send,
    c_recv,
    d_send,
    d_recv,
    own_buf,
    hg_buf,
    probe_buf,
    target_buf,
    err_buf,
    l1_send,
    l1_recv,
    l2_send,
    l2_recv,
    g_send,
    g_recv,
    ag_buf,
    in_sem,
    w_sem,
    out_sem,
    entry_sem,
    a_sems,
    c_sems,
    d_sems,
    l1_sems,
    l2_sems,
    rs_ssem,
    rs_rsem,
    ag_ssem,
    ag_rsem,
):
    prompts = k_ref.shape[0]
    tokens, features = q_ref.shape
    local_heads = features // HDIM
    classes = probe_ref.shape[0]
    block = res_buf.shape[1]
    d = lax.axis_index("dp")
    t = lax.axis_index("tensor")
    core = lax.rem(t, 2)
    sib = t + 1 - 2 * core
    opp = lax.rem(t + 2, 4)
    opp_sib = lax.rem(sib + 2, 4)
    partner = lax.rem(d + n_dp // 2, n_dp)

    barrier = pltpu.get_barrier_semaphore()
    pl.semaphore_signal(barrier, inc=1, device_id=(d, sib), device_id_type=MESH)
    pl.semaphore_signal(barrier, inc=1, device_id=(d, opp), device_id_type=MESH)
    for off in range(1, n_dp):
        pl.semaphore_signal(
            barrier, inc=1, device_id=(lax.rem(d + off, n_dp), t), device_id_type=MESH
        )

    in_copies = []
    for place, (source, target) in enumerate(
        (
            (patch_hbm, patch_ref),
            (q_hbm, q_ref),
            (k_hbm, k_ref),
            (v_hbm, v_ref),
            (slot_hbm, slot_ref),
            (label_hbm, label_ref),
            (probe_hbm, probe_ref),
            (gain_hbm, gain_ref),
            (residual_hbm, res_buf),
        )
    ):
        copy = pltpu.make_async_copy(source, target, in_sem.at[place])
        in_copies.append(copy)
    w_copies = []
    for place, owner in enumerate((opp_sib, opp, sib, t)):
        columns = pl.ds(pl.multiple_of(owner * block, block), block)
        copy = pltpu.make_async_copy(
            weight_hbm.at[:, columns], w_buf.at[place], w_sem.at[place]
        )
        w_copies.append(copy)
    for copy in in_copies[:8] + w_copies + in_copies[8:]:
        copy.start()

    rows = local_heads * length
    spots = lax.broadcasted_iota(jnp.int32, (rows, patch_ref.shape[2]), 0)

    def one_hot(j):
        pairs = patch_ref[j]
        row = (pairs[0:1, :] - t * local_heads) * length + pairs[1:2, :]
        return jnp.where(spots == row, 1.0, 0.0).astype(BF16)

    def queries_of(j):
        low = j * length
        return jnp.concatenate(
            [
                q_ref[low : low + length, h * HDIM : (h + 1) * HDIM]
                for h in range(local_heads)
            ],
            axis=0,
        )

    def weights_of(scores, causal):
        scores = jnp.where(causal, scores * (1.0 / math.sqrt(HDIM)), -jnp.inf)
        exponent = jnp.exp(scores - jnp.max(scores, axis=0, keepdims=True))
        total = jnp.sum(exponent, axis=0, keepdims=True)
        return (exponent * (1.0 / total)).astype(BF16)

    every = range(prompts)
    entries = patch_ref.shape[2]
    picks = lax.broadcasted_iota(jnp.int32, (entries, rows), 1)

    def one_hot_rows(j):
        return jnp.where(picks == columns_of[:, j : j + 1], 1.0, 0.0).astype(BF16)

    for copy in in_copies[:4]:
        copy.wait()
    index_rows = jnp.concatenate(
        [(patch_ref[j][0:1, :] - t * local_heads) * length + patch_ref[j][1:2, :] for j in every],
        axis=0,
    )
    wide = jnp.concatenate(
        [index_rows, jnp.zeros((prompts, LANES - entries), jnp.int32)], axis=1
    )
    columns_of = wide.T[:entries, :]
    picked = [contract(one_hot_rows(j), queries_of(j), 1, 0).astype(BF16) for j in every]
    scores = [contract(k_ref[j], picked[j], 1, 1) for j in every]
    s_id = lax.broadcasted_iota(jnp.int32, scores[0].shape, 0)
    weights = [weights_of(scores[j], s_id <= patch_ref[j][1:2, :]) for j in every]
    for j in every:
        entry_send[j] = contract(weights[j], v_ref[j], 0, 0).astype(BF16)

    pl.semaphore_wait(barrier, n_dp + 1)
    entry_copy = pltpu.make_async_remote_copy(
        src_ref=entry_send,
        dst_ref=entry_recv,
        send_sem=entry_sem.at[0],
        recv_sem=entry_sem.at[1],
        device_id=(partner, t),
        device_id_type=MESH,
    )
    entry_copy.start()

    s_id = lax.broadcasted_iota(jnp.int32, (length, rows), 0)
    i_id = lax.rem(lax.broadcasted_iota(jnp.int32, (length, rows), 1), length)
    causal = s_id <= i_id

    def attend(low, high):
        some = range(low, high)
        scores = [contract(k_ref[j], queries_of(j), 1, 1) for j in some]
        weights = [weights_of(part, causal) for part in scores]
        for j, part in zip(some, weights):
            heads_buf[j] = contract(part, v_ref[j], 0, 0).astype(BF16)

    ready = min(4, prompts)
    for low in range(0, ready, 2):
        attend(low, min(low + 2, ready))
    in_copies[4].wait()
    entry_copy.wait()

    def patch(j):
        arrived = entry_recv[slot_ref[j]]
        both = jnp.concatenate([arrived, jnp.ones_like(arrived)], axis=1)
        placed = contract(one_hot(j), both, 1, 0)
        patched = jnp.where(
            placed[:, HDIM:] > 0.5, placed[:, :HDIM], heads_buf[j].astype(F32)
        ).astype(BF16)
        for h in range(local_heads):
            x_buf[chunk(j), h * HDIM : (h + 1) * HDIM] = patched[
                h * length : (h + 1) * length
            ]

    def chunk(j):
        return pl.ds(pl.multiple_of(j * length, length), length)

    def remote(source, target, sems, j, device, place=None):
        place = chunk(j) if place is None else place
        return pltpu.make_async_remote_copy(
            src_ref=source.at[place],
            dst_ref=target.at[place],
            send_sem=sems.at[0, j],
            recv_sem=sems.at[1, j],
            device_id=(d, device),
            device_id_type=MESH,
        )

    def project(rows, place):
        return jnp.dot(x_buf[rows, :], w_buf[place], preferred_element_type=F32).astype(BF16)

    def start_a(j):
        a_send[chunk(j), :] = project(chunk(j), 0)
        remote(a_send, a_recv, a_sems, j, sib).start()

    def start_c(j):
        mine = project(chunk(j), 1).astype(F32)
        remote(a_send, a_recv, a_sems, j, sib).wait()
        c_send[chunk(j), :] = (mine + a_recv[chunk(j), :].astype(F32)).astype(BF16)
        remote(c_send, c_recv, c_sems, j, opp).start()

    patch(0)
    w_copies[0].wait()
    start_a(0)
    w_copies[1].wait()

    def first(j, carry):
        patch(j + 1)
        start_a(j + 1)
        start_c(j)
        return carry

    done = 0
    for low in range(ready, prompts, 2):
        first(done, 0)
        done += 1
        attend(low, min(low + 2, prompts))
    lax.fori_loop(done, prompts - 1, first, 0)
    start_c(prompts - 1)
    w_copies[2].wait()
    w_copies[3].wait()
    halves = d_sems.shape[1]
    half = tokens // halves

    def d_copy(j):
        place = pl.ds(pl.multiple_of(j * half, half), half)
        return remote(d_send, d_recv, d_sems, j, sib, place)

    def second(j, carry):
        place = pl.ds(pl.multiple_of(j * half, half), half)
        d_send[place, :] = project(place, 2)
        d_copy(j).start()
        own_buf[place, :] = project(place, 3)
        return carry

    lax.fori_loop(0, halves, second, 0)
    for copy in in_copies[5:]:
        copy.wait()
    probe = probe_ref[...].astype(BF16)
    probe_buf[...] = jnp.concatenate([probe, jnp.zeros_like(probe)], axis=0)
    for j in every:
        class_id = lax.broadcasted_iota(jnp.int32, (classes, length), 0)
        target = jnp.where(class_id == label_ref[j : j + 1, :], 1.0, 0.0)
        target_buf[j] = target.T
    for j in range(halves):
        d_copy(j).wait()

    def pack(part, squares):
        lane = lax.broadcasted_iota(jnp.int32, part.shape, 1)
        high = squares.astype(BF16).astype(F32)
        part = jnp.where(lane == classes, high, part)
        part = jnp.where(lane == classes + 1, squares - high, part)
        return part.astype(BF16)

    def unpack(message):
        message = message.astype(F32)
        lane = lax.broadcasted_iota(jnp.int32, message.shape, 1)
        tail = jnp.where((lane == classes) | (lane == classes + 1), message, 0.0)
        return message, jnp.sum(tail, axis=1, keepdims=True)

    def stage3(j):
        remote(c_send, c_recv, c_sems, j, opp).wait()
        at = chunk(j)
        own = own_buf[at, :].astype(F32) + d_recv[at, :].astype(F32)
        attn = (own + c_recv[at, :].astype(F32)).astype(BF16)
        out_buf[at, :] = attn
        hidden = res_buf[at, :].astype(F32) + attn.astype(F32)
        squares = jnp.sum(hidden * hidden, axis=1, keepdims=True)
        hg = (hidden * gain_ref[...]).astype(BF16)
        hg_buf[at, :] = hg
        part = contract(hg, probe_buf[...], 1, 1)
        l1_send[j] = pack(part, squares)
        remote(l1_send, l1_recv, l1_sems, j, sib, j).start()

    def stage4(j):
        remote(l1_send, l1_recv, l1_sems, j, sib, j).wait()
        part_a, squares_a = unpack(l1_send[j])
        part_b, squares_b = unpack(l1_recv[j])
        l2_send[j] = pack(part_a + part_b, squares_a + squares_b)
        remote(l2_send, l2_recv, l2_sems, j, opp, j).start()

    def stage5(low, high):
        for j in range(low, high):
            remote(l2_send, l2_recv, l2_sems, j, opp, j).wait()
        count = (high - low) * length
        part_a, squares_a = unpack(l2_send[low:high].reshape(count, LANES))
        part_b, squares_b = unpack(l2_recv[low:high].reshape(count, LANES))
        inverse = lax.rsqrt((squares_a + squares_b) / width + norm_epsilon)
        logits = (part_a + part_b)[:, :classes] * inverse
        logits_ref[low:high] = logits.reshape(high - low, length, classes)
        error = jax.nn.sigmoid(logits) - target_buf[low:high].reshape(count, classes)
        err_buf[low * length : high * length, :] = (error * inverse).astype(BF16)

    out_copies = [
        pltpu.make_async_copy(source, target, out_sem.at[place])
        for place, (source, target) in enumerate(
            ((out_buf, out_hbm), (logits_ref, logits_hbm), (grad_ref, grad_hbm))
        )
    ]
    stage3(0)

    def third(j, carry):
        stage3(j)
        stage4(j - 1)
        return carry

    lax.fori_loop(1, prompts, third, 0)
    out_copies[0].start()
    last = prompts - 1
    stage4(last)
    stage5(0, last)
    early = last * length
    grad = contract(err_buf[:early, :], hg_buf[:early, :], 0, 0)
    stage5(last, prompts)
    out_copies[1].start()
    grad = grad + contract(err_buf[early:, :], hg_buf[early:, :], 0, 0)

    piece_rows = g_send.shape[1]
    per_column = classes // piece_rows
    for i in range(n_dp):
        column, row = i // per_column * LANES, i % per_column * piece_rows
        g_send[i] = grad[row : row + piece_rows, column : column + LANES].astype(g_send.dtype)

    def scatter(peer_to, peer_from):
        return pltpu.make_async_remote_copy(
            src_ref=g_send.at[peer_to],
            dst_ref=g_recv.at[peer_from],
            send_sem=rs_ssem.at[peer_to],
            recv_sem=rs_rsem.at[peer_from],
            device_id=(peer_to, t),
            device_id_type=MESH,
        )

    def gather(peer_to, piece):
        return pltpu.make_async_remote_copy(
            src_ref=ag_buf.at[piece],
            dst_ref=ag_buf.at[piece],
            send_sem=ag_ssem.at[peer_to],
            recv_sem=ag_rsem.at[piece],
            device_id=(peer_to, t),
            device_id_type=MESH,
        )

    peers = [lax.rem(d + off, n_dp) for off in range(1, n_dp)]
    for peer in peers:
        scatter(peer, d).start()
    g_recv[d] = g_send[d]
    for peer in peers:
        scatter(peer, peer).wait_recv()
    total = g_recv[0].astype(F32)
    for i in range(1, n_dp):
        total = total + g_recv[i].astype(F32)
    ag_buf[d] = (total * (1.0 / math.sqrt(tokens * n_dp))).astype(ag_buf.dtype)
    for peer in peers:
        gather(peer, d).start()
    for peer in peers:
        gather(peer, peer).wait_recv()
    for i in range(n_dp):
        column, row = i // per_column * LANES, i % per_column * piece_rows
        grad_ref[row : row + piece_rows, column : column + LANES] = ag_buf[i].astype(F32)
    out_copies[2].start()
    for peer in peers:
        scatter(peer, peer).wait_send()
        gather(peer, d).wait_send()
    for copy in out_copies:
        copy.wait()


def store_kernel(count, *refs):
    sources, targets, held = refs[:count], refs[count : 2 * count], refs[2 * count : -2]
    load_sems, store_sems = refs[-2:]
    parts = []
    for source, target, buffer in zip(sources, targets, held):
        step = source.shape[0] // STORE_PARTS
        for i in range(STORE_PARTS):
            at = pl.ds(i * step, step)
            place = len(parts)
            load = pltpu.make_async_copy(
                source.at[at], buffer.at[at], load_sems.at[place]
            )
            store = pltpu.make_async_copy(
                buffer.at[at], target.at[at], store_sems.at[place]
            )
            parts.append((load, store))
    for load, _ in parts:
        load.start()
    for load, store in parts:
        load.wait()
        store.start()
    for _, store in parts:
        store.wait()


def per_device(
    residual,
    queries,
    attn_keys,
    values,
    out_weight,
    norm_gain,
    probe_weight,
    partner_slot,
    patch_list,
    concept_labels,
):
    n_dp = lax.axis_size("dp")
    prompts, length, block = residual.shape
    width = out_weight.shape[1]
    features = queries.shape[2]
    classes = probe_weight.shape[1]
    entries = patch_list.shape[1]
    rows = features // HDIM * length
    tokens = prompts * length
    piece_rows = classes * block // LANES // n_dp
    piece_type = BF16 if piece_rows % 16 == 0 else F32
    anywhere = pl.BlockSpec(memory_space=pl.ANY)
    dma = pltpu.SemaphoreType.DMA
    part = pltpu.VMEM((tokens, block), BF16)
    message = pltpu.VMEM((prompts, length, LANES), BF16)
    pieces = pltpu.VMEM((n_dp, piece_rows, LANES), piece_type)
    scratch = [
        pltpu.SMEM((prompts,), jnp.int32),
        pltpu.VMEM((tokens, features), BF16),
        pltpu.VMEM(attn_keys.shape, BF16),
        pltpu.VMEM(values.shape, BF16),
        pltpu.VMEM((prompts, 2, entries), jnp.int32),
        pltpu.VMEM(concept_labels.shape, jnp.int32),
        pltpu.VMEM((1, block), F32),
        pltpu.VMEM((classes, block), F32),
        pltpu.VMEM((4, features, block), BF16),
        part,
        part,
        pltpu.VMEM((prompts, length, classes), F32),
        pltpu.VMEM((classes, block), F32),
        pltpu.VMEM((prompts, rows, HDIM), BF16),
        pltpu.VMEM((tokens, features), BF16),
        pltpu.VMEM((prompts, entries, HDIM), BF16),
        pltpu.VMEM((prompts, entries, HDIM), BF16),
        part,
        part,
        part,
        part,
        part,
        part,
        part,
        part,
        pltpu.VMEM((2 * classes, block), BF16),
        pltpu.VMEM((prompts, length, classes), F32),
        pltpu.VMEM((tokens, classes), BF16),
        message,
        message,
        message,
        message,
        pieces,
        pieces,
        pieces,
        dma((9,)),
        dma((4,)),
        dma((3,)),
        dma((2,)),
        dma((2, prompts)),
        dma((2, prompts)),
        dma((2, 2)),
        dma((2, prompts)),
        dma((2, prompts)),
        dma((n_dp,)),
        dma((n_dp,)),
        dma((n_dp,)),
        dma((n_dp,)),
    ]
    results = (
        jax.ShapeDtypeStruct((tokens, block), BF16),
        jax.ShapeDtypeStruct((prompts, length, classes), F32),
        jax.ShapeDtypeStruct((classes, block), F32),
    )
    held = pl.pallas_call(
        functools.partial(kernel, n_dp, width, length),
        out_shape=results,
        in_specs=[anywhere] * 10,
        out_specs=(anywhere,) * 3,
        scratch_shapes=scratch,
        compiler_params=pltpu.CompilerParams(
            collective_id=0, has_side_effects=True, vmem_limit_bytes=VMEM_BYTES
        ),
    )(
        partner_slot,
        queries.reshape(tokens, features),
        attn_keys,
        values,
        jnp.swapaxes(patch_list, 1, 2),
        concept_labels,
        norm_gain.reshape(1, block),
        probe_weight.T,
        out_weight,
        residual.reshape(tokens, block),
    )
    attn_out, logits, grad = pl.pallas_call(
        functools.partial(store_kernel, len(results)),
        out_shape=results,
        in_specs=[anywhere] * 3,
        out_specs=(anywhere,) * 3,
        scratch_shapes=[pltpu.VMEM(result.shape, result.dtype) for result in results]
        + [dma((len(results) * STORE_PARTS,))] * 2,
        compiler_params=pltpu.CompilerParams(vmem_limit_bytes=VMEM_BYTES),
    )(*held)
    return attn_out.reshape(prompts, length, block), logits, grad.T


def solution(mesh):
    return jax.shard_map(
        per_device,
        mesh=mesh,
        in_specs=(
            P("dp", None, "tensor"),
            P("dp", None, "tensor"),
            P("dp", None, "tensor"),
            P("dp", None, "tensor"),
            P("tensor", None),
            P("tensor"),
            P("tensor", None),
            P("dp"),
            P("dp", "tensor", None),
            P("dp", None),
        ),
        out_specs=(P("dp", None, "tensor"), P("dp", None, None), P("tensor", None)),
        check_vma=False,
    )
```

```python
import functools
import math

import jax
import jax.numpy as jnp
from jax import lax
from jax.experimental import pallas as pl
from jax.experimental.pallas import tpu as pltpu
from jax.sharding import PartitionSpec as P

HDIM = 128
LANES = 128
STORE_PARTS = 2
VMEM_BYTES = 62 * 1024 * 1024
norm_epsilon = 1e-05
MESH = pl.DeviceIdType.MESH
F32 = jnp.float32
BF16 = jnp.bfloat16


def contract(a, b, dim_a, dim_b):
    return lax.dot_general(
        a, b, (((dim_a,), (dim_b,)), ((), ())), preferred_element_type=F32
    )


def kernel(
    n_dp,
    width,
    length,
    slot_hbm,
    q_hbm,
    k_hbm,
    v_hbm,
    patch_hbm,
    label_hbm,
    gain_hbm,
    probe_hbm,
    weight_hbm,
    residual_hbm,
    out_hbm,
    logits_hbm,
    grad_hbm,
    slot_ref,
    q_ref,
    k_ref,
    v_ref,
    patch_ref,
    label_ref,
    gain_ref,
    probe_ref,
    w_buf,
    res_buf,
    out_buf,
    logits_ref,
    grad_ref,
    heads_buf,
    x_buf,
    entry_send,
    entry_recv,
    a_send,
    a_recv,
    c_send,
    c_recv,
    d_send,
    d_recv,
    own_buf,
    hg_buf,
    probe_buf,
    target_buf,
    err_buf,
    l1_send,
    l1_recv,
    l2_send,
    l2_recv,
    g_send,
    g_recv,
    ag_buf,
    in_sem,
    w_sem,
    out_sem,
    entry_sem,
    a_sems,
    c_sems,
    d_sems,
    l1_sems,
    l2_sems,
    rs_ssem,
    rs_rsem,
    ag_ssem,
    ag_rsem,
):
    prompts = k_ref.shape[0]
    tokens, features = q_ref.shape
    local_heads = features // HDIM
    classes = probe_ref.shape[0]
    block = res_buf.shape[1]
    d = lax.axis_index("dp")
    t = lax.axis_index("tensor")
    core = lax.rem(t, 2)
    sib = t + 1 - 2 * core
    opp = lax.rem(t + 2, 4)
    opp_sib = lax.rem(sib + 2, 4)
    partner = lax.rem(d + n_dp // 2, n_dp)

    barrier = pltpu.get_barrier_semaphore()
    pl.semaphore_signal(barrier, inc=1, device_id=(d, sib), device_id_type=MESH)
    pl.semaphore_signal(barrier, inc=1, device_id=(d, opp), device_id_type=MESH)
    for off in range(1, n_dp):
        pl.semaphore_signal(
            barrier, inc=1, device_id=(lax.rem(d + off, n_dp), t), device_id_type=MESH
        )

    in_copies = []
    for place, (source, target) in enumerate(
        (
            (patch_hbm, patch_ref),
            (q_hbm, q_ref),
            (k_hbm, k_ref),
            (v_hbm, v_ref),
            (slot_hbm, slot_ref),
            (label_hbm, label_ref),
            (probe_hbm, probe_ref),
            (gain_hbm, gain_ref),
            (residual_hbm, res_buf),
        )
    ):
        copy = pltpu.make_async_copy(source, target, in_sem.at[place])
        in_copies.append(copy)
    w_copies = []
    for place, owner in enumerate((opp_sib, opp, sib, t)):
        columns = pl.ds(pl.multiple_of(owner * block, block), block)
        copy = pltpu.make_async_copy(
            weight_hbm.at[:, columns], w_buf.at[place], w_sem.at[place]
        )
        w_copies.append(copy)
    for copy in in_copies[:8]:
        copy.start()

    rows = local_heads * length
    spots = lax.broadcasted_iota(jnp.int32, (rows, patch_ref.shape[2]), 0)

    def one_hot(j):
        pairs = patch_ref[j]
        row = (pairs[0:1, :] - t * local_heads) * length + pairs[1:2, :]
        return jnp.where(spots == row, 1.0, 0.0).astype(BF16)

    def queries_of(j):
        low = j * length
        return jnp.concatenate(
            [
                q_ref[low : low + length, h * HDIM : (h + 1) * HDIM]
                for h in range(local_heads)
            ],
            axis=0,
        )

    def weights_of(scores, causal):
        scores = jnp.where(causal, scores * (1.0 / math.sqrt(HDIM)), -jnp.inf)
        exponent = jnp.exp(scores - jnp.max(scores, axis=0, keepdims=True))
        total = jnp.sum(exponent, axis=0, keepdims=True)
        return (exponent * (1.0 / total)).astype(BF16)

    every = range(prompts)
    entries = patch_ref.shape[2]
    picks = lax.broadcasted_iota(jnp.int32, (entries, rows), 1)

    def one_hot_rows(j):
        return jnp.where(picks == columns_of[:, j : j + 1], 1.0, 0.0).astype(BF16)

    for copy in in_copies[:4]:
        copy.wait()
    for copy in w_copies + in_copies[8:]:
        copy.start()
    index_rows = jnp.concatenate(
        [(patch_ref[j][0:1, :] - t * local_heads) * length + patch_ref[j][1:2, :] for j in every],
        axis=0,
    )
    wide = jnp.concatenate(
        [index_rows, jnp.zeros((prompts, LANES - entries), jnp.int32)], axis=1
    )
    columns_of = wide.T[:entries, :]
    picked = [contract(one_hot_rows(j), queries_of(j), 1, 0).astype(BF16) for j in every]
    scores = [contract(k_ref[j], picked[j], 1, 1) for j in every]
    s_id = lax.broadcasted_iota(jnp.int32, scores[0].shape, 0)
    weights = [weights_of(scores[j], s_id <= patch_ref[j][1:2, :]) for j in every]
    for j in every:
        entry_send[j] = contract(weights[j], v_ref[j], 0, 0).astype(BF16)

    pl.semaphore_wait(barrier, n_dp + 1)
    entry_copy = pltpu.make_async_remote_copy(
        src_ref=entry_send,
        dst_ref=entry_recv,
        send_sem=entry_sem.at[0],
        recv_sem=entry_sem.at[1],
        device_id=(partner, t),
        device_id_type=MESH,
    )
    entry_copy.start()

    s_id = lax.broadcasted_iota(jnp.int32, (length, rows), 0)
    i_id = lax.rem(lax.broadcasted_iota(jnp.int32, (length, rows), 1), length)
    causal = s_id <= i_id

    def attend(low, high):
        some = range(low, high)
        scores = [contract(k_ref[j], queries_of(j), 1, 1) for j in some]
        weights = [weights_of(part, causal) for part in scores]
        for j, part in zip(some, weights):
            heads_buf[j] = contract(part, v_ref[j], 0, 0).astype(BF16)

    ready = min(4, prompts)
    for low in range(0, ready, 2):
        attend(low, min(low + 2, ready))
    in_copies[4].wait()
    entry_copy.wait()

    def patch(j):
        arrived = entry_recv[slot_ref[j]]
        both = jnp.concatenate([arrived, jnp.ones_like(arrived)], axis=1)
        placed = contract(one_hot(j), both, 1, 0)
        patched = jnp.where(
            placed[:, HDIM:] > 0.5, placed[:, :HDIM], heads_buf[j].astype(F32)
        ).astype(BF16)
        for h in range(local_heads):
            x_buf[chunk(j), h * HDIM : (h + 1) * HDIM] = patched[
                h * length : (h + 1) * length
            ]

    def chunk(j):
        return pl.ds(pl.multiple_of(j * length, length), length)

    def remote(source, target, sems, j, device, place=None):
        place = chunk(j) if place is None else place
        return pltpu.make_async_remote_copy(
            src_ref=source.at[place],
            dst_ref=target.at[place],
            send_sem=sems.at[0, j],
            recv_sem=sems.at[1, j],
            device_id=(d, device),
            device_id_type=MESH,
        )

    def project(rows, place):
        return jnp.dot(x_buf[rows, :], w_buf[place], preferred_element_type=F32).astype(BF16)

    def rows_of(low, high):
        return slice(low * length, high * length)

    def start_a(low, high):
        a_send[rows_of(low, high), :] = project(rows_of(low, high), 0)
        for j in range(low, high):
            remote(a_send, a_recv, a_sems, j, sib).start()

    def start_c(low, high):
        at = rows_of(low, high)
        mine = project(at, 1).astype(F32)
        for j in range(low, high):
            remote(a_send, a_recv, a_sems, j, sib).wait()
        c_send[at, :] = (mine + a_recv[at, :].astype(F32)).astype(BF16)
        for j in range(low, high):
            remote(c_send, c_recv, c_sems, j, opp).start()

    groups = [(0, 1), (1, 2)] + [
        (low, min(low + 2, prompts)) for low in range(2, prompts, 2)
    ]
    waiting = list(range(ready, prompts, 2))
    for place, (low, high) in enumerate(groups):
        for j in range(low, high):
            patch(j)
        if place < 2:
            w_copies[place].wait()
        start_a(low, high)
        if place > 0:
            start_c(*groups[place - 1])
            if waiting:
                attend(waiting[0], min(waiting[0] + 2, prompts))
                waiting.pop(0)
    start_c(*groups[-1])
    w_copies[2].wait()
    w_copies[3].wait()
    halves = d_sems.shape[1]
    half = tokens // halves

    def d_copy(j):
        place = pl.ds(pl.multiple_of(j * half, half), half)
        return remote(d_send, d_recv, d_sems, j, sib, place)

    def second(j, carry):
        place = pl.ds(pl.multiple_of(j * half, half), half)
        d_send[place, :] = project(place, 2)
        d_copy(j).start()
        own_buf[place, :] = project(place, 3)
        return carry

    lax.fori_loop(0, halves, second, 0)
    for copy in in_copies[5:]:
        copy.wait()
    probe = probe_ref[...]
    probe_buf[...] = jnp.concatenate([probe, jnp.zeros_like(probe)], axis=0).T.astype(BF16)
    for j in every:
        class_id = lax.broadcasted_iota(jnp.int32, (classes, length), 0)
        target = jnp.where(class_id == label_ref[j : j + 1, :], 1.0, 0.0)
        target_buf[j] = target.T
    for j in range(halves):
        d_copy(j).wait()

    def pack(part, squares):
        lane = lax.broadcasted_iota(jnp.int32, part.shape, 1)
        high = squares.astype(BF16).astype(F32)
        part = jnp.where(lane == classes, high, part)
        part = jnp.where(lane == classes + 1, squares - high, part)
        return part.astype(BF16)

    def unpack(message):
        message = message.astype(F32)
        lane = lax.broadcasted_iota(jnp.int32, message.shape, 1)
        tail = jnp.where((lane == classes) | (lane == classes + 1), message, 0.0)
        return message, jnp.sum(tail, axis=1, keepdims=True)

    def stage3(j):
        remote(c_send, c_recv, c_sems, j, opp).wait()
        at = chunk(j)
        own = own_buf[at, :].astype(F32) + d_recv[at, :].astype(F32)
        attn = (own + c_recv[at, :].astype(F32)).astype(BF16)
        out_buf[at, :] = attn
        hidden = res_buf[at, :].astype(F32) + attn.astype(F32)
        squares = jnp.sum(hidden * hidden, axis=1, keepdims=True)
        hg = (hidden * gain_ref[...]).astype(BF16)
        hg_buf[at, :] = hg
        part = contract(hg, probe_buf[...], 1, 0)
        l1_send[j] = pack(part, squares)
        remote(l1_send, l1_recv, l1_sems, j, sib, j).start()

    def stage4(j):
        remote(l1_send, l1_recv, l1_sems, j, sib, j).wait()
        part_a, squares_a = unpack(l1_send[j])
        part_b, squares_b = unpack(l1_recv[j])
        l2_send[j] = pack(part_a + part_b, squares_a + squares_b)
        remote(l2_send, l2_recv, l2_sems, j, opp, j).start()

    def stage5(low, high):
        for j in range(low, high):
            remote(l2_send, l2_recv, l2_sems, j, opp, j).wait()
        count = (high - low) * length
        part_a, squares_a = unpack(l2_send[low:high].reshape(count, LANES))
        part_b, squares_b = unpack(l2_recv[low:high].reshape(count, LANES))
        inverse = lax.rsqrt((squares_a + squares_b) / width + norm_epsilon)
        logits = (part_a + part_b)[:, :classes] * inverse
        logits_ref[low:high] = logits.reshape(high - low, length, classes)
        error = jax.nn.sigmoid(logits) - target_buf[low:high].reshape(count, classes)
        err_buf[low * length : high * length, :] = (error * inverse).astype(BF16)

    out_copies = [
        pltpu.make_async_copy(source, target, out_sem.at[place])
        for place, (source, target) in enumerate(
            ((out_buf, out_hbm), (logits_ref, logits_hbm), (grad_ref, grad_hbm))
        )
    ]
    stage3(0)

    def third(j, carry):
        stage3(j)
        stage4(j - 1)
        return carry

    lax.fori_loop(1, prompts, third, 0)
    out_copies[0].start()
    last = prompts - 1
    stage4(last)
    stage5(0, last)
    early = last * length
    grad = contract(err_buf[:early, :], hg_buf[:early, :], 0, 0)
    stage5(last, prompts)
    out_copies[1].start()
    grad = grad + contract(err_buf[early:, :], hg_buf[early:, :], 0, 0)

    piece_rows = g_send.shape[1]
    per_column = classes // piece_rows
    for i in range(n_dp):
        column, row = i // per_column * LANES, i % per_column * piece_rows
        g_send[i] = grad[row : row + piece_rows, column : column + LANES].astype(g_send.dtype)

    def scatter(peer_to, peer_from):
        return pltpu.make_async_remote_copy(
            src_ref=g_send.at[peer_to],
            dst_ref=g_recv.at[peer_from],
            send_sem=rs_ssem.at[peer_to],
            recv_sem=rs_rsem.at[peer_from],
            device_id=(peer_to, t),
            device_id_type=MESH,
        )

    def gather(peer_to, piece):
        return pltpu.make_async_remote_copy(
            src_ref=ag_buf.at[piece],
            dst_ref=ag_buf.at[piece],
            send_sem=ag_ssem.at[peer_to],
            recv_sem=ag_rsem.at[piece],
            device_id=(peer_to, t),
            device_id_type=MESH,
        )

    peers = [lax.rem(d + off, n_dp) for off in range(1, n_dp)]
    for peer in peers:
        scatter(peer, d).start()
    g_recv[d] = g_send[d]
    for peer in peers:
        scatter(peer, peer).wait_recv()
    total = g_recv[0].astype(F32)
    for i in range(1, n_dp):
        total = total + g_recv[i].astype(F32)
    ag_buf[d] = (total * (1.0 / math.sqrt(tokens * n_dp))).astype(ag_buf.dtype)
    for peer in peers:
        gather(peer, d).start()
    for peer in peers:
        gather(peer, peer).wait_recv()
    for i in range(n_dp):
        column, row = i // per_column * LANES, i % per_column * piece_rows
        grad_ref[row : row + piece_rows, column : column + LANES] = ag_buf[i].astype(F32)
    out_copies[2].start()
    for peer in peers:
        scatter(peer, peer).wait_send()
        gather(peer, d).wait_send()
    for copy in out_copies:
        copy.wait()


def store_kernel(count, *refs):
    sources, targets, held = refs[:count], refs[count : 2 * count], refs[2 * count : -2]
    load_sems, store_sems = refs[-2:]
    parts = []
    for source, target, buffer in zip(sources, targets, held):
        step = source.shape[0] // STORE_PARTS
        for i in range(STORE_PARTS):
            at = pl.ds(i * step, step)
            place = len(parts)
            load = pltpu.make_async_copy(
                source.at[at], buffer.at[at], load_sems.at[place]
            )
            store = pltpu.make_async_copy(
                buffer.at[at], target.at[at], store_sems.at[place]
            )
            parts.append((load, store))
    for load, _ in parts:
        load.start()
    for load, store in parts:
        load.wait()
        store.start()
    for _, store in parts:
        store.wait()


def per_device(
    residual,
    queries,
    attn_keys,
    values,
    out_weight,
    norm_gain,
    probe_weight,
    partner_slot,
    patch_list,
    concept_labels,
):
    n_dp = lax.axis_size("dp")
    prompts, length, block = residual.shape
    width = out_weight.shape[1]
    features = queries.shape[2]
    classes = probe_weight.shape[1]
    entries = patch_list.shape[1]
    rows = features // HDIM * length
    tokens = prompts * length
    piece_rows = classes * block // LANES // n_dp
    piece_type = BF16 if piece_rows % 16 == 0 else F32
    anywhere = pl.BlockSpec(memory_space=pl.ANY)
    dma = pltpu.SemaphoreType.DMA
    part = pltpu.VMEM((tokens, block), BF16)
    message = pltpu.VMEM((prompts, length, LANES), BF16)
    pieces = pltpu.VMEM((n_dp, piece_rows, LANES), piece_type)
    scratch = [
        pltpu.SMEM((prompts,), jnp.int32),
        pltpu.VMEM((tokens, features), BF16),
        pltpu.VMEM(attn_keys.shape, BF16),
        pltpu.VMEM(values.shape, BF16),
        pltpu.VMEM((prompts, 2, entries), jnp.int32),
        pltpu.VMEM(concept_labels.shape, jnp.int32),
        pltpu.VMEM((1, block), F32),
        pltpu.VMEM((classes, block), F32),
        pltpu.VMEM((4, features, block), BF16),
        part,
        part,
        pltpu.VMEM((prompts, length, classes), F32),
        pltpu.VMEM((classes, block), F32),
        pltpu.VMEM((prompts, rows, HDIM), BF16),
        pltpu.VMEM((tokens, features), BF16),
        pltpu.VMEM((prompts, entries, HDIM), BF16),
        pltpu.VMEM((prompts, entries, HDIM), BF16),
        part,
        part,
        part,
        part,
        part,
        part,
        part,
        part,
        pltpu.VMEM((block, 2 * classes), BF16),
        pltpu.VMEM((prompts, length, classes), F32),
        pltpu.VMEM((tokens, classes), BF16),
        message,
        message,
        message,
        message,
        pieces,
        pieces,
        pieces,
        dma((9,)),
        dma((4,)),
        dma((3,)),
        dma((2,)),
        dma((2, prompts)),
        dma((2, prompts)),
        dma((2, 2)),
        dma((2, prompts)),
        dma((2, prompts)),
        dma((n_dp,)),
        dma((n_dp,)),
        dma((n_dp,)),
        dma((n_dp,)),
    ]
    results = (
        jax.ShapeDtypeStruct((tokens, block), BF16),
        jax.ShapeDtypeStruct((prompts, length, classes), F32),
        jax.ShapeDtypeStruct((classes, block), F32),
    )
    held = pl.pallas_call(
        functools.partial(kernel, n_dp, width, length),
        out_shape=results,
        in_specs=[anywhere] * 10,
        out_specs=(anywhere,) * 3,
        scratch_shapes=scratch,
        compiler_params=pltpu.CompilerParams(
            collective_id=0, has_side_effects=True, vmem_limit_bytes=VMEM_BYTES
        ),
    )(
        partner_slot,
        queries.reshape(tokens, features),
        attn_keys,
        values,
        jnp.swapaxes(patch_list, 1, 2),
        concept_labels,
        norm_gain.reshape(1, block),
        probe_weight.T,
        out_weight,
        residual.reshape(tokens, block),
    )
    attn_out, logits, grad = pl.pallas_call(
        functools.partial(store_kernel, len(results)),
        out_shape=results,
        in_specs=[anywhere] * 3,
        out_specs=(anywhere,) * 3,
        scratch_shapes=[pltpu.VMEM(result.shape, result.dtype) for result in results]
        + [dma((len(results) * STORE_PARTS,))] * 2,
        compiler_params=pltpu.CompilerParams(vmem_limit_bytes=VMEM_BYTES),
    )(*held)
    return attn_out.reshape(prompts, length, block), logits, grad.T


def solution(mesh):
    return jax.shard_map(
        per_device,
        mesh=mesh,
        in_specs=(
            P("dp", None, "tensor"),
            P("dp", None, "tensor"),
            P("dp", None, "tensor"),
            P("dp", None, "tensor"),
            P("tensor", None),
            P("tensor"),
            P("tensor", None),
            P("dp"),
            P("dp", "tensor", None),
            P("dp", None),
        ),
        out_specs=(P("dp", None, "tensor"), P("dp", None, None), P("tensor", None)),
        check_vma=False,
    )
```

```python
import functools
import math

import jax
import jax.numpy as jnp
from jax import lax
from jax.experimental import pallas as pl
from jax.experimental.pallas import tpu as pltpu
from jax.sharding import PartitionSpec as P

HDIM = 128
LANES = 128
STORE_PARTS = 2
VMEM_BYTES = 62 * 1024 * 1024
norm_epsilon = 1e-05
MESH = pl.DeviceIdType.MESH
F32 = jnp.float32
BF16 = jnp.bfloat16


def contract(a, b, dim_a, dim_b):
    return lax.dot_general(
        a, b, (((dim_a,), (dim_b,)), ((), ())), preferred_element_type=F32
    )


def kernel(
    n_dp,
    width,
    length,
    slot_hbm,
    q_hbm,
    k_hbm,
    v_hbm,
    patch_hbm,
    label_hbm,
    gain_hbm,
    probe_hbm,
    weight_hbm,
    residual_hbm,
    out_hbm,
    logits_hbm,
    grad_hbm,
    slot_ref,
    q_ref,
    k_ref,
    v_ref,
    patch_ref,
    label_ref,
    gain_ref,
    probe_ref,
    w_buf,
    res_buf,
    out_buf,
    logits_ref,
    grad_ref,
    heads_buf,
    x_buf,
    entry_send,
    entry_recv,
    a_send,
    a_recv,
    c_send,
    c_recv,
    d_send,
    d_recv,
    own_buf,
    hg_buf,
    probe_buf,
    target_buf,
    err_buf,
    l1_send,
    l1_recv,
    l2_send,
    l2_recv,
    cross_recv,
    g_send,
    g_recv,
    ag_buf,
    in_sem,
    w_sem,
    out_sem,
    entry_sem,
    a_sems,
    c_sems,
    d_sems,
    l1_sems,
    l2_sems,
    cross_sem,
    rs_ssem,
    rs_rsem,
    ag_ssem,
    ag_rsem,
):
    prompts = k_ref.shape[0]
    tokens, features = q_ref.shape
    local_heads = features // HDIM
    classes = probe_ref.shape[0]
    block = res_buf.shape[1]
    d = lax.axis_index("dp")
    t = lax.axis_index("tensor")
    core = lax.rem(t, 2)
    sib = t + 1 - 2 * core
    opp = lax.rem(t + 2, 4)
    opp_sib = lax.rem(sib + 2, 4)
    partner = lax.rem(d + n_dp // 2, n_dp)

    barrier = pltpu.get_barrier_semaphore()
    pl.semaphore_signal(barrier, inc=1, device_id=(d, sib), device_id_type=MESH)
    pl.semaphore_signal(barrier, inc=1, device_id=(d, opp), device_id_type=MESH)
    pl.semaphore_signal(barrier, inc=1, device_id=(d, opp_sib), device_id_type=MESH)
    for off in range(1, n_dp):
        pl.semaphore_signal(
            barrier, inc=1, device_id=(lax.rem(d + off, n_dp), t), device_id_type=MESH
        )

    in_copies = []
    for place, (source, target) in enumerate(
        (
            (patch_hbm, patch_ref),
            (q_hbm, q_ref),
            (k_hbm, k_ref),
            (v_hbm, v_ref),
            (slot_hbm, slot_ref),
            (label_hbm, label_ref),
            (probe_hbm, probe_ref),
            (gain_hbm, gain_ref),
            (residual_hbm, res_buf),
        )
    ):
        copy = pltpu.make_async_copy(source, target, in_sem.at[place])
        in_copies.append(copy)
    w_copies = []
    for place, owner in enumerate((opp_sib, opp, sib, t)):
        columns = pl.ds(pl.multiple_of(owner * block, block), block)
        copy = pltpu.make_async_copy(
            weight_hbm.at[:, columns], w_buf.at[place], w_sem.at[place]
        )
        w_copies.append(copy)
    for copy in in_copies[:8]:
        copy.start()

    rows = local_heads * length
    spots = lax.broadcasted_iota(jnp.int32, (rows, patch_ref.shape[2]), 0)

    def one_hot(j):
        pairs = patch_ref[j]
        row = (pairs[0:1, :] - t * local_heads) * length + pairs[1:2, :]
        return jnp.where(spots == row, 1.0, 0.0).astype(BF16)

    def queries_of(j):
        low = j * length
        return jnp.concatenate(
            [
                q_ref[low : low + length, h * HDIM : (h + 1) * HDIM]
                for h in range(local_heads)
            ],
            axis=0,
        )

    def weights_of(scores, causal):
        scores = jnp.where(causal, scores * (1.0 / math.sqrt(HDIM)), -jnp.inf)
        exponent = jnp.exp(scores - jnp.max(scores, axis=0, keepdims=True))
        total = jnp.sum(exponent, axis=0, keepdims=True)
        return (exponent * (1.0 / total)).astype(BF16)

    every = range(prompts)
    entries = patch_ref.shape[2]
    picks = lax.broadcasted_iota(jnp.int32, (entries, rows), 1)

    def one_hot_rows(j):
        return jnp.where(picks == columns_of[:, j : j + 1], 1.0, 0.0).astype(BF16)

    for copy in in_copies[:4]:
        copy.wait()
    for copy in w_copies + in_copies[8:]:
        copy.start()
    index_rows = jnp.concatenate(
        [(patch_ref[j][0:1, :] - t * local_heads) * length + patch_ref[j][1:2, :] for j in every],
        axis=0,
    )
    wide = jnp.concatenate(
        [index_rows, jnp.zeros((prompts, LANES - entries), jnp.int32)], axis=1
    )
    columns_of = wide.T[:entries, :]
    picked = [contract(one_hot_rows(j), queries_of(j), 1, 0).astype(BF16) for j in every]
    scores = [contract(k_ref[j], picked[j], 1, 1) for j in every]
    s_id = lax.broadcasted_iota(jnp.int32, scores[0].shape, 0)
    weights = [weights_of(scores[j], s_id <= patch_ref[j][1:2, :]) for j in every]
    for j in every:
        entry_send[j] = contract(weights[j], v_ref[j], 0, 0).astype(BF16)

    pl.semaphore_wait(barrier, n_dp + 2)
    entry_copy = pltpu.make_async_remote_copy(
        src_ref=entry_send,
        dst_ref=entry_recv,
        send_sem=entry_sem.at[0],
        recv_sem=entry_sem.at[1],
        device_id=(partner, t),
        device_id_type=MESH,
    )
    entry_copy.start()

    s_id = lax.broadcasted_iota(jnp.int32, (length, rows), 0)
    i_id = lax.rem(lax.broadcasted_iota(jnp.int32, (length, rows), 1), length)
    causal = s_id <= i_id

    def attend(low, high):
        some = range(low, high)
        scores = [contract(k_ref[j], queries_of(j), 1, 1) for j in some]
        weights = [weights_of(part, causal) for part in scores]
        for j, part in zip(some, weights):
            heads_buf[j] = contract(part, v_ref[j], 0, 0).astype(BF16)

    ready = min(4, prompts)
    for low in range(0, ready, 2):
        attend(low, min(low + 2, ready))
    in_copies[4].wait()
    entry_copy.wait()

    def patch(j):
        arrived = entry_recv[slot_ref[j]]
        both = jnp.concatenate([arrived, jnp.ones_like(arrived)], axis=1)
        placed = contract(one_hot(j), both, 1, 0)
        patched = jnp.where(
            placed[:, HDIM:] > 0.5, placed[:, :HDIM], heads_buf[j].astype(F32)
        ).astype(BF16)
        for h in range(local_heads):
            x_buf[chunk(j), h * HDIM : (h + 1) * HDIM] = patched[
                h * length : (h + 1) * length
            ]

    def chunk(j):
        return pl.ds(pl.multiple_of(j * length, length), length)

    def remote(source, target, sems, j, device, place=None):
        place = chunk(j) if place is None else place
        return pltpu.make_async_remote_copy(
            src_ref=source.at[place],
            dst_ref=target.at[place],
            send_sem=sems.at[0, j],
            recv_sem=sems.at[1, j],
            device_id=(d, device),
            device_id_type=MESH,
        )

    def project(rows, place):
        return jnp.dot(x_buf[rows, :], w_buf[place], preferred_element_type=F32).astype(BF16)

    def rows_of(low, high):
        return slice(low * length, high * length)

    def start_a(low, high):
        a_send[rows_of(low, high), :] = project(rows_of(low, high), 0)
        for j in range(low, high):
            remote(a_send, a_recv, a_sems, j, sib).start()

    def start_c(low, high):
        at = rows_of(low, high)
        mine = project(at, 1).astype(F32)
        for j in range(low, high):
            remote(a_send, a_recv, a_sems, j, sib).wait()
        c_send[at, :] = (mine + a_recv[at, :].astype(F32)).astype(BF16)
        for j in range(low, high):
            remote(c_send, c_recv, c_sems, j, opp).start()

    groups = [(0, 1), (1, 2)] + [
        (low, min(low + 2, prompts)) for low in range(2, prompts, 2)
    ]
    waiting = list(range(ready, prompts, 2))
    for place, (low, high) in enumerate(groups):
        for j in range(low, high):
            patch(j)
        if place < 2:
            w_copies[place].wait()
        start_a(low, high)
        if place > 0:
            start_c(*groups[place - 1])
            if waiting:
                attend(waiting[0], min(waiting[0] + 2, prompts))
                waiting.pop(0)
    start_c(*groups[-1])
    w_copies[2].wait()
    w_copies[3].wait()
    halves = d_sems.shape[1]
    half = tokens // halves

    def d_copy(j):
        place = pl.ds(pl.multiple_of(j * half, half), half)
        return remote(d_send, d_recv, d_sems, j, sib, place)

    def second(j, carry):
        place = pl.ds(pl.multiple_of(j * half, half), half)
        d_send[place, :] = project(place, 2)
        d_copy(j).start()
        own_buf[place, :] = project(place, 3)
        return carry

    lax.fori_loop(0, halves, second, 0)
    for copy in in_copies[5:]:
        copy.wait()
    probe = probe_ref[...]
    probe_buf[...] = jnp.concatenate([probe, jnp.zeros_like(probe)], axis=0).T.astype(BF16)
    for j in every:
        class_id = lax.broadcasted_iota(jnp.int32, (classes, length), 0)
        target = jnp.where(class_id == label_ref[j : j + 1, :], 1.0, 0.0)
        target_buf[j] = target.T
    for j in range(halves):
        d_copy(j).wait()

    def pack(part, squares):
        lane = lax.broadcasted_iota(jnp.int32, part.shape, 1)
        high = squares.astype(BF16).astype(F32)
        part = jnp.where(lane == classes, high, part)
        part = jnp.where(lane == classes + 1, squares - high, part)
        return part.astype(BF16)

    def unpack(message):
        message = message.astype(F32)
        lane = lax.broadcasted_iota(jnp.int32, message.shape, 1)
        tail = jnp.where((lane == classes) | (lane == classes + 1), message, 0.0)
        return message, jnp.sum(tail, axis=1, keepdims=True)

    def stage3(j):
        remote(c_send, c_recv, c_sems, j, opp).wait()
        at = chunk(j)
        own = own_buf[at, :].astype(F32) + d_recv[at, :].astype(F32)
        attn = (own + c_recv[at, :].astype(F32)).astype(BF16)
        out_buf[at, :] = attn
        hidden = res_buf[at, :].astype(F32) + attn.astype(F32)
        squares = jnp.sum(hidden * hidden, axis=1, keepdims=True)
        hg = (hidden * gain_ref[...]).astype(BF16)
        hg_buf[at, :] = hg
        part = contract(hg, probe_buf[...], 1, 0)
        l1_send[j] = pack(part, squares)
        remote(l1_send, l1_recv, l1_sems, j, sib, j).start()

    def stage4(j):
        remote(l1_send, l1_recv, l1_sems, j, sib, j).wait()
        part_a, squares_a = unpack(l1_send[j])
        part_b, squares_b = unpack(l1_recv[j])
        l2_send[j] = pack(part_a + part_b, squares_a + squares_b)
        remote(l2_send, l2_recv, l2_sems, j, opp, j).start()

    def direct_copies(j):
        return (
            pltpu.make_async_remote_copy(
                src_ref=l1_send.at[j],
                dst_ref=l2_recv.at[j],
                send_sem=l2_sems.at[0, j],
                recv_sem=l2_sems.at[1, j],
                device_id=(d, opp),
                device_id_type=MESH,
            ),
            pltpu.make_async_remote_copy(
                src_ref=l1_send.at[j],
                dst_ref=cross_recv,
                send_sem=cross_sem.at[0],
                recv_sem=cross_sem.at[1],
                device_id=(d, opp_sib),
                device_id_type=MESH,
            ),
        )

    def add(one, two):
        return one[0] + two[0], one[1] + two[1]

    def stage5(low, high, here, there):
        count = (high - low) * length
        part_a, squares_a = here
        part_b, squares_b = there
        inverse = lax.rsqrt((squares_a + squares_b) / width + norm_epsilon)
        logits = (part_a + part_b)[:, :classes] * inverse
        logits_ref[low:high] = logits.reshape(high - low, length, classes)
        error = jax.nn.sigmoid(logits) - target_buf[low:high].reshape(count, classes)
        err_buf[low * length : high * length, :] = (error * inverse).astype(BF16)

    out_copies = [
        pltpu.make_async_copy(source, target, out_sem.at[place])
        for place, (source, target) in enumerate(
            ((out_buf, out_hbm), (logits_ref, logits_hbm), (grad_ref, grad_hbm))
        )
    ]
    stage3(0)

    def third(j, carry):
        stage3(j)
        stage4(j - 1)
        return carry

    lax.fori_loop(1, prompts, third, 0)
    out_copies[0].start()
    last = prompts - 1
    direct = direct_copies(last)
    for copy in direct:
        copy.start()
    for j in range(last):
        remote(l2_send, l2_recv, l2_sems, j, opp, j).wait()
    early = last * length
    stage5(
        0,
        last,
        unpack(l2_send[:last].reshape(early, LANES)),
        unpack(l2_recv[:last].reshape(early, LANES)),
    )
    grad = contract(err_buf[:early, :], hg_buf[:early, :], 0, 0)
    remote(l1_send, l1_recv, l1_sems, last, sib, last).wait()
    for copy in direct:
        copy.wait()
    stage5(
        last,
        prompts,
        add(unpack(l1_send[last]), unpack(l1_recv[last])),
        add(unpack(l2_recv[last]), unpack(cross_recv[...])),
    )
    out_copies[1].start()
    grad = grad + contract(err_buf[early:, :], hg_buf[early:, :], 0, 0)

    piece_rows = g_send.shape[1]
    per_column = classes // piece_rows
    for i in range(n_dp):
        column, row = i // per_column * LANES, i % per_column * piece_rows
        g_send[i] = grad[row : row + piece_rows, column : column + LANES].astype(g_send.dtype)

    def scatter(peer_to, peer_from):
        return pltpu.make_async_remote_copy(
            src_ref=g_send.at[peer_to],
            dst_ref=g_recv.at[peer_from],
            send_sem=rs_ssem.at[peer_to],
            recv_sem=rs_rsem.at[peer_from],
            device_id=(peer_to, t),
            device_id_type=MESH,
        )

    def gather(peer_to, piece):
        return pltpu.make_async_remote_copy(
            src_ref=ag_buf.at[piece],
            dst_ref=ag_buf.at[piece],
            send_sem=ag_ssem.at[peer_to],
            recv_sem=ag_rsem.at[piece],
            device_id=(peer_to, t),
            device_id_type=MESH,
        )

    offsets = sorted(range(1, n_dp), key=lambda off: abs(off - n_dp // 2))
    peers = [lax.rem(d + off, n_dp) for off in offsets]
    for peer in peers:
        scatter(peer, d).start()
    g_recv[d] = g_send[d]
    for peer in peers:
        scatter(peer, peer).wait_recv()
    total = g_recv[0].astype(F32)
    for i in range(1, n_dp):
        total = total + g_recv[i].astype(F32)
    ag_buf[d] = (total * (1.0 / math.sqrt(tokens * n_dp))).astype(ag_buf.dtype)
    for peer in peers:
        gather(peer, d).start()
    for peer in peers:
        gather(peer, peer).wait_recv()
    for i in range(n_dp):
        column, row = i // per_column * LANES, i % per_column * piece_rows
        grad_ref[row : row + piece_rows, column : column + LANES] = ag_buf[i].astype(F32)
    out_copies[2].start()
    for peer in peers:
        scatter(peer, peer).wait_send()
        gather(peer, d).wait_send()
    for copy in out_copies:
        copy.wait()


def store_kernel(count, *refs):
    sources, targets, held = refs[:count], refs[count : 2 * count], refs[2 * count : -2]
    load_sems, store_sems = refs[-2:]
    parts = []
    for source, target, buffer in zip(sources, targets, held):
        step = source.shape[0] // STORE_PARTS
        for i in range(STORE_PARTS):
            at = pl.ds(i * step, step)
            place = len(parts)
            load = pltpu.make_async_copy(
                source.at[at], buffer.at[at], load_sems.at[place]
            )
            store = pltpu.make_async_copy(
                buffer.at[at], target.at[at], store_sems.at[place]
            )
            parts.append((load, store))
    for load, _ in parts:
        load.start()
    for load, store in parts:
        load.wait()
        store.start()
    for _, store in parts:
        store.wait()


def per_device(
    residual,
    queries,
    attn_keys,
    values,
    out_weight,
    norm_gain,
    probe_weight,
    partner_slot,
    patch_list,
    concept_labels,
):
    n_dp = lax.axis_size("dp")
    prompts, length, block = residual.shape
    width = out_weight.shape[1]
    features = queries.shape[2]
    classes = probe_weight.shape[1]
    entries = patch_list.shape[1]
    rows = features // HDIM * length
    tokens = prompts * length
    piece_rows = classes * block // LANES // n_dp
    piece_type = BF16 if piece_rows % 16 == 0 else F32
    anywhere = pl.BlockSpec(memory_space=pl.ANY)
    dma = pltpu.SemaphoreType.DMA
    part = pltpu.VMEM((tokens, block), BF16)
    message = pltpu.VMEM((prompts, length, LANES), BF16)
    pieces = pltpu.VMEM((n_dp, piece_rows, LANES), piece_type)
    scratch = [
        pltpu.SMEM((prompts,), jnp.int32),
        pltpu.VMEM((tokens, features), BF16),
        pltpu.VMEM(attn_keys.shape, BF16),
        pltpu.VMEM(values.shape, BF16),
        pltpu.VMEM((prompts, 2, entries), jnp.int32),
        pltpu.VMEM(concept_labels.shape, jnp.int32),
        pltpu.VMEM((1, block), F32),
        pltpu.VMEM((classes, block), F32),
        pltpu.VMEM((4, features, block), BF16),
        part,
        part,
        pltpu.VMEM((prompts, length, classes), F32),
        pltpu.VMEM((classes, block), F32),
        pltpu.VMEM((prompts, rows, HDIM), BF16),
        pltpu.VMEM((tokens, features), BF16),
        pltpu.VMEM((prompts, entries, HDIM), BF16),
        pltpu.VMEM((prompts, entries, HDIM), BF16),
        part,
        part,
        part,
        part,
        part,
        part,
        part,
        part,
        pltpu.VMEM((block, 2 * classes), BF16),
        pltpu.VMEM((prompts, length, classes), F32),
        pltpu.VMEM((tokens, classes), BF16),
        message,
        message,
        message,
        message,
        pltpu.VMEM((length, LANES), BF16),
        pieces,
        pieces,
        pieces,
        dma((9,)),
        dma((4,)),
        dma((3,)),
        dma((2,)),
        dma((2, prompts)),
        dma((2, prompts)),
        dma((2, 2)),
        dma((2, prompts)),
        dma((2, prompts)),
        dma((2,)),
        dma((n_dp,)),
        dma((n_dp,)),
        dma((n_dp,)),
        dma((n_dp,)),
    ]
    results = (
        jax.ShapeDtypeStruct((tokens, block), BF16),
        jax.ShapeDtypeStruct((prompts, length, classes), F32),
        jax.ShapeDtypeStruct((classes, block), F32),
    )
    held = pl.pallas_call(
        functools.partial(kernel, n_dp, width, length),
        out_shape=results,
        in_specs=[anywhere] * 10,
        out_specs=(anywhere,) * 3,
        scratch_shapes=scratch,
        compiler_params=pltpu.CompilerParams(
            collective_id=0, has_side_effects=True, vmem_limit_bytes=VMEM_BYTES
        ),
    )(
        partner_slot,
        queries.reshape(tokens, features),
        attn_keys,
        values,
        jnp.swapaxes(patch_list, 1, 2),
        concept_labels,
        norm_gain.reshape(1, block),
        probe_weight.T,
        out_weight,
        residual.reshape(tokens, block),
    )
    attn_out, logits, grad = pl.pallas_call(
        functools.partial(store_kernel, len(results)),
        out_shape=results,
        in_specs=[anywhere] * 3,
        out_specs=(anywhere,) * 3,
        scratch_shapes=[pltpu.VMEM(result.shape, result.dtype) for result in results]
        + [dma((len(results) * STORE_PARTS,))] * 2,
        compiler_params=pltpu.CompilerParams(vmem_limit_bytes=VMEM_BYTES),
    )(*held)
    return attn_out.reshape(prompts, length, block), logits, grad.T


def solution(mesh):
    return jax.shard_map(
        per_device,
        mesh=mesh,
        in_specs=(
            P("dp", None, "tensor"),
            P("dp", None, "tensor"),
            P("dp", None, "tensor"),
            P("dp", None, "tensor"),
            P("tensor", None),
            P("tensor"),
            P("tensor", None),
            P("dp"),
            P("dp", "tensor", None),
            P("dp", None),
        ),
        out_specs=(P("dp", None, "tensor"), P("dp", None, None), P("tensor", None)),
        check_vma=False,
    )
```
